512 devices in a mesh: ctx: 64 (over x, z), head: 8 (over y, core).
Axes of the slice: x: 4, y: 4, z: 16, core: 2. Of those that a mesh axis runs over, the one named last changes fastest.
Arguments:
- queries: bfloat16 [65536, 2048], P('ctx', 'head'), may hold values from -6 to 6
- lin_keys: bfloat16 [65536, 2048], P('ctx', 'head'), may hold values from -6 to 6
- lin_values: bfloat16 [65536, 2048], P('ctx', 'head'), may hold values from -6 to 6
- level_class: int32 [65536], P('ctx'), may hold values from 0 to 15
- level_table: float32 [16, 16, 11], P(None, 'head'), may hold values from 0.25 to 4
- win_keys: bfloat16 [65536, 512], P(('ctx', 'head')), may hold values from -6 to 6
- win_values: bfloat16 [65536, 512], P(('ctx', 'head')), may hold values from -6 to 6
- seg_ids: int32 [65536], P(('ctx', 'head')), may hold values from 0 to 255, never falling along the last dimension, each value on 1 to 2048 neighbouring positions
Outputs:
- mixed_heads: bfloat16 [65536, 2048], P('ctx', 'head')
- window_out: bfloat16 [65536, 2048], P(('ctx', 'head'))
The draws below stay inside these ranges and needn't reach their ends.
Inputs may be any that keep to these rules, and one draw needn't show every extreme that they name: `seg_ids`: document numbers never fall along the tokens; each document has 1 to 2048 tokens and one has exactly 2048.
All inputs are finite; a program needn't handle non-finite values.
Results may differ from the reference program's by a relative error of at most 0.0085.
Values may be sent and summed in bfloat16 or wider, within the bound.
No kernel may reach another device: no remote copies, remote signals or barrier semaphores. Data moves between devices by JAX's collectives and lax.ppermute only.
A program may use at most 128 MiB of HBM per device.

```python
import math
import jax
import jax.numpy as jnp
import numpy as np
from jax import lax

H = 16
E = 128
KVH = 4
TOK_DEV = 1024
BLK = 64
W = 256
NCLASS = 16
TOKENS = 65536
LEVELS = 11
SEGS = 256
SEGMAX = 2048
N_CTX = 64


def shared_factors(key):
    factor_key = jax.random.fold_in(key, 4177)
    key_fac, key_kpat, key_vmag, key_vsign = jax.random.split(factor_key, 4)
    factors = 1.1 * jnp.clip(jax.random.normal(key_fac, (TOKENS, 2), jnp.float32), -3.0, 3.0)
    key_pattern = jax.random.uniform(key_kpat, (2, H * E), jnp.float32, 0.4, 1.2)
    value_mag = jax.random.uniform(key_vmag, (2, H * E), jnp.float32, 0.6, 1.4)
    value_sign = jnp.where(jax.random.bernoulli(key_vsign, 0.5, (2, H * E)), 1.0, -1.0)
    return (factors, key_pattern, value_mag * value_sign)


def apply_factors(factors, pattern):
    return factors[:, 0:1] * pattern[0][None, :] + factors[:, 1:2] * pattern[1][None, :]


def draw_queries(key, part):
    key_base = jax.random.fold_in(key, 11)
    drawn = jnp.clip(jax.random.normal(key_base, (TOKENS, H * E), jnp.float32), -6.0, 6.0)
    return drawn.astype(jnp.bfloat16)


def draw_lin_keys(key, part):
    factors, key_pattern, value_pattern = shared_factors(key)
    key_off, key_noise = jax.random.split(jax.random.fold_in(key, 29))
    span_count = TOKENS // TOK_DEV
    offset = jax.random.uniform(key_off, (span_count, H), jnp.float32, -2.5, 2.5)
    offset_cols = jnp.repeat(offset, E, axis=1)
    token_noise = jnp.clip(jax.random.normal(key_noise, (TOKENS, H * E), jnp.float32), -2.0, 2.0)
    drawn = jnp.repeat(offset_cols, TOK_DEV, axis=0) + token_noise + apply_factors(factors, key_pattern)
    return jnp.clip(drawn, -6.0, 6.0).astype(jnp.bfloat16)


def draw_win_keys(key, part):
    key_base = jax.random.fold_in(key, 13)
    drawn = jnp.clip(jax.random.normal(key_base, (TOKENS, KVH * E), jnp.float32), -6.0, 6.0)
    return drawn.astype(jnp.bfloat16)


def draw_lin_values(key, part):
    factors, key_pattern, value_pattern = shared_factors(key)
    key_mean, key_noise, key_cols = jax.random.split(jax.random.fold_in(key, 23), 3)
    span_count = TOKENS // TOK_DEV
    key_mag, key_sign = jax.random.split(key_cols)
    col_mag = jax.random.uniform(key_mag, (H * E,), jnp.float32, 0.6, 1.4)
    col_sign = jnp.where(jax.random.bernoulli(key_sign, 0.5, (H * E,)), 1.0, -1.0)
    parity = jnp.where(jnp.arange(span_count) % 2 == 0, 1.0, -1.0).astype(jnp.float32)
    span_rough = 0.5 * jnp.clip(jax.random.normal(key_mean, (span_count, H * E), jnp.float32), -2.0, 2.0)
    span_mean = 2.0 * parity[:, None] * (col_mag * col_sign)[None, :] + span_rough
    token_noise = jnp.clip(jax.random.normal(key_noise, (TOKENS, H * E), jnp.float32), -2.0, 2.0)
    drawn = jnp.repeat(span_mean, TOK_DEV, axis=0) + token_noise + apply_factors(factors, value_pattern)
    return jnp.clip(drawn, -6.0, 6.0).astype(jnp.bfloat16)


def place_ends(array, rng, smallest, high):
    dims = array.shape
    place = [jax.random.randint(jax.random.fold_in(rng, axis), (), 0, dims[axis]) for axis in range(len(dims))]
    array = array.at[tuple(place)].set(smallest)
    longest = dims.index(max(dims))
    place[longest] = (place[longest] + 1) % dims[longest]
    return array.at[tuple(place)].set(high)


def shard_levels(own_key, dims, shards, smallest, top_value):
    loudness = 1.0
    for dim, parts in shards:
        steps = jax.random.uniform(jax.random.fold_in(jax.random.fold_in(own_key, 6), dim), (parts,), jnp.float32, smallest / len(shards), top_value / len(shards))
        loudness = loudness * jnp.repeat(jnp.exp(steps), dims[dim] // parts).reshape((-1,) + (1,) * (len(dims) - 1 - dim))
    return loudness


def split_up(number_of, total, most, slope):
    weights = [(1 << 20) // math.isqrt(rank ** slope) + 1 for rank in range(2, number_of + 1)]
    rest, counts = total - most - (number_of - 1), [1] * (number_of - 1)
    while rest > 0:
        free = [i for i in range(number_of - 1) if counts[i] < most]
        mass, left = sum([weights[i] for i in free]), rest
        for i in free:
            more = min(most - counts[i], max(1, left * weights[i] // mass), rest)
            counts[i] = counts[i] + more
            rest = rest - more
    return np.array([most] + counts)


def ragged_sizes(key, amount, total, most, slope):
    if amount == 2:
        one = jax.random.randint(key, (), max(1, total - most), min(most, total - 1) + 1)
        return jnp.stack([one, total - one])
    tallies = jnp.asarray(split_up(amount, total, most, slope), jnp.int32)
    pairs = (amount - 1) // 2
    source_of, receiver = tallies[1:1 + 2 * pairs:2], tallies[2:2 + 2 * pairs:2]
    slack = jnp.minimum(source_of - 1, most - receiver)
    moved = jax.random.randint(jax.random.fold_in(key, 1), (pairs,), 0, 1 << 20) % (slack + 1)
    tallies = tallies.at[1:1 + 2 * pairs:2].set(source_of - moved).at[2:2 + 2 * pairs:2].set(receiver + moved)
    return tallies[jax.random.permutation(jax.random.fold_in(key, 2), amount)]


def scatter_about(key, shape, deviation, bound, pieces=(), held_as=jnp.bfloat16):
    level = shard_levels(key, shape, pieces, -0.22, 0.18) if pieces else 1.0
    values = jax.random.normal(key, shape, jnp.float32) * deviation * level
    return jnp.minimum(jnp.maximum(values, -bound), bound).astype(held_as)


def setup_inputs(seed: int = 0) -> dict:
    key_list = jax.random.split(jax.random.key(seed), 9)
    queries = draw_queries(jax.random.fold_in(key_list[8], 71), 0)
    lin_keys = draw_lin_keys(jax.random.fold_in(key_list[8], 71), 0)
    lin_values = draw_lin_values(jax.random.fold_in(key_list[8], 71), 0)
    level_class = place_ends(jax.random.randint(key_list[3], (TOKENS,), 0, NCLASS), jax.random.fold_in(key_list[3], 1), 0, NCLASS - 1).astype(jnp.int32)
    level_table = jnp.clip(jnp.exp(math.log(4.0) - 2.7725887 * jax.random.uniform(key_list[4], (NCLASS, H, LEVELS), jnp.float32) ** shard_levels(key_list[4], (NCLASS, H, LEVELS), ((1, 8),), -0.2, 0.2)), 0.25, 4.0)
    win_keys = draw_win_keys(jax.random.fold_in(key_list[8], 71), 0)
    win_values = scatter_about(key_list[6], (TOKENS, KVH * E), 1.0, 6.0, ((0, 512),))
    seg_ids = jnp.searchsorted(jnp.cumsum(ragged_sizes(key_list[7], SEGS, TOKENS, SEGMAX, 1)), jnp.arange(TOKENS), side="right").astype(jnp.int32)
    return {"queries": queries, "lin_keys": lin_keys, "lin_values": lin_values, "level_class": level_class, "level_table": level_table, "win_keys": win_keys, "win_values": win_values, "seg_ids": seg_ids}


HIGHEST_PREC = lax.Precision.HIGHEST


def top_bit(values, width):
    counted = jnp.zeros(values.shape, jnp.int32)
    for bit_num in range(width):
        counted = counted + (values >= (1 << bit_num)).astype(jnp.int32)
    return counted


def reference(queries, lin_keys, lin_values, level_class, level_table, win_keys, win_values, seg_ids):
    span_bits = (TOK_DEV // BLK).bit_length() - 1
    ctx_bits = N_CTX.bit_length() - 1
    local_levels = span_bits + 1
    q_feats = (1.0 + jax.nn.elu(queries.astype(jnp.float32))).astype(jnp.bfloat16).reshape(N_CTX, TOK_DEV, H, E)
    k_feats = (1.0 + jax.nn.elu(lin_keys.astype(jnp.float32))).astype(jnp.bfloat16).reshape(N_CTX, TOK_DEV, H, E)
    v_heads = lin_values.reshape(N_CTX, TOK_DEV, H, E)

    def span_state(inputs):
        k_span, v_span = inputs
        k_wide = k_span.astype(jnp.float32)
        state_now = jnp.einsum("sha,shb->hab", k_wide, v_span.astype(jnp.float32), precision=HIGHEST_PREC)
        return state_now, jnp.sum(k_wide, axis=0)

    states, key_sums = lax.map(span_state, (k_feats, v_heads))
    span_ids = jnp.arange(N_CTX, dtype=jnp.int32)
    pair_level = top_bit(jnp.bitwise_xor(span_ids[:, None], span_ids[None, :]), ctx_bits) - 1
    below = span_ids[None, :] < span_ids[:, None]
    level_ids = jnp.arange(ctx_bits, dtype=jnp.int32)
    picked = ((pair_level[:, :, None] == level_ids[None, None, :]) & below[:, :, None]).astype(jnp.float32)
    tok_ids = jnp.arange(TOK_DEV, dtype=jnp.int32)
    block_ids = tok_ids // BLK
    inner_level = top_bit(jnp.bitwise_xor(block_ids[:, None], block_ids[None, :]), span_bits)
    causal = tok_ids[None, :] <= tok_ids[:, None]
    class_spans = level_class.reshape(N_CTX, TOK_DEV)

    def span_out(inputs):
        q_span, k_span, v_span, class_span, pick_span = inputs
        level_weight = jnp.transpose(level_table[class_span], (1, 0, 2))
        bucket = jnp.einsum("jl,jhab->lhab", pick_span, states, precision=HIGHEST_PREC)
        bucket_sum = jnp.einsum("jl,jha->lha", pick_span, key_sums, precision=HIGHEST_PREC)
        q_wide = q_span.astype(jnp.float32)
        scores = jnp.einsum("tha,sha->hts", q_wide, k_span.astype(jnp.float32), precision=HIGHEST_PREC)
        scores = jnp.where(causal[None], scores, 0.0)
        inner_den = jnp.stack([jnp.sum(jnp.where(inner_level == level_num, scores, 0.0), axis=-1) for level_num in range(local_levels)], axis=-1)
        outer_den = jnp.einsum("tha,lha->htl", q_wide, bucket_sum, precision=HIGHEST_PREC)
        coeffs = level_weight / jnp.maximum(jnp.concatenate([inner_den, outer_den], axis=-1), 1.0)
        weight = jnp.zeros(scores.shape, jnp.float32)
        for level_num in range(local_levels):
            weight = weight + jnp.where(inner_level == level_num, coeffs[:, :, level_num:level_num + 1], 0.0)
        weight = (weight * scores).astype(jnp.bfloat16)
        inner_part = jnp.einsum("hts,shb->thb", weight.astype(jnp.float32), v_span.astype(jnp.float32), precision=HIGHEST_PREC)
        through = jnp.einsum("tha,lhab->htlb", q_wide, bucket, precision=HIGHEST_PREC)
        outer_part = jnp.einsum("htlb,htl->thb", through, coeffs[:, :, local_levels:], precision=HIGHEST_PREC)
        return (inner_part + outer_part).astype(jnp.bfloat16)

    mixed_heads = lax.map(span_out, (q_feats, k_feats, v_heads, class_spans, picked)).reshape(TOKENS, H * E)

    gate_scale = 0.5 + jax.nn.sigmoid(mixed_heads.astype(jnp.float32))
    queries_gated = (queries.astype(jnp.float32) * gate_scale).astype(jnp.bfloat16)
    group_size = H // KVH
    keys_pad = jnp.concatenate([jnp.zeros((W, KVH * E), win_keys.dtype), win_keys], axis=0)
    values_pad = jnp.concatenate([jnp.zeros((W, KVH * E), win_values.dtype), win_values], axis=0)
    segs_pad = jnp.concatenate([jnp.full((W,), -1, jnp.int32), seg_ids.astype(jnp.int32)], axis=0)
    rows_blk = math.gcd(TOKENS, 512)

    def window_block(first_row):
        q_blk = lax.dynamic_slice_in_dim(queries_gated, first_row, rows_blk, 0).astype(jnp.float32).reshape(rows_blk, KVH, group_size, E)
        k_blk = lax.dynamic_slice_in_dim(keys_pad, first_row, rows_blk + W, 0).astype(jnp.float32).reshape(rows_blk + W, KVH, E)
        v_blk = lax.dynamic_slice_in_dim(values_pad, first_row, rows_blk + W, 0).astype(jnp.float32).reshape(rows_blk + W, KVH, E)
        seg_keys = lax.dynamic_slice_in_dim(segs_pad, first_row, rows_blk + W, 0)
        seg_rows = lax.dynamic_slice_in_dim(seg_ids.astype(jnp.int32), first_row, rows_blk, 0)
        q_pos = first_row + jnp.arange(rows_blk, dtype=jnp.int32)
        k_pos = first_row - W + jnp.arange(rows_blk + W, dtype=jnp.int32)
        allowed = (k_pos[None, :] <= q_pos[:, None]) & (k_pos[None, :] > q_pos[:, None] - W) & (seg_keys[None, :] == seg_rows[:, None])
        scores = jnp.einsum("tkga,ska->kgts", q_blk, k_blk, precision=HIGHEST_PREC) * (E ** -0.5)
        row_max = jnp.max(jnp.where(allowed, scores, -jnp.inf), axis=-1, keepdims=True)
        exp_scores = jnp.exp(jnp.where(allowed, scores - row_max, -jnp.inf))
        weights_bf = (exp_scores / jnp.sum(exp_scores, axis=-1, keepdims=True)).astype(jnp.bfloat16)
        out_rows = jnp.einsum("kgts,skb->tkgb", weights_bf.astype(jnp.float32), v_blk, precision=HIGHEST_PREC)
        return out_rows.reshape(rows_blk, H * E).astype(jnp.bfloat16)

    starts = jnp.arange(TOKENS // rows_blk, dtype=jnp.int32) * rows_blk
    window_out = lax.map(window_block, starts).reshape(TOKENS, H * E)
    return (mixed_heads, window_out)
```

```python
import functools

import jax
import jax.numpy as jnp
from jax import lax
from jax.experimental import pallas as pl
from jax.experimental.pallas import tpu as pltpu
from jax.sharding import Mesh
from jax.sharding import PartitionSpec as P

H = 16
E = 128
KVH = 4
NCLASS = 16
HEADS = 2
TOK = 1024
TILE = 128
SUMS = HEADS * E
ROWS = SUMS + 16
F32 = jnp.float32
BF16 = jnp.bfloat16
LOG2E = 1.4426950408889634


def feats(x):
    x = x.astype(F32)
    return jnp.where(x > 0, x + 1.0, jnp.exp(x)).astype(BF16)


def dot_nn(a, b):
    return lax.dot_general(a, b, (((1,), (0,)), ((), ())), preferred_element_type=F32)


def dot_nt(a, b):
    return lax.dot_general(a, b, (((1,), (1,)), ((), ())), preferred_element_type=F32)


def dot_tn(a, b):
    return lax.dot_general(a, b, (((0,), (0,)), ((), ())), preferred_element_type=F32)


def hi_lo(x):
    hi = x.astype(BF16)
    return hi, (x - hi.astype(F32)).astype(BF16)


def head_cols(h):
    return slice(h * E, (h + 1) * E)


def sum_rows(sums):
    row = lax.broadcasted_iota(jnp.int32, (16, E), 0)
    out = jnp.zeros((16, E), F32)
    for h in range(HEADS):
        hi = sums[h].astype(BF16).astype(F32)
        out = jnp.where(row == h, hi, out)
        out = jnp.where(row == HEADS + h, sums[h] - hi, out)
    return out.astype(BF16)


def state_kernel(k_ref, v_ref, s_ref):
    sums = []
    for h in range(HEADS):
        kf = feats(k_ref[:, head_cols(h)])
        state = dot_tn(kf, v_ref[:, head_cols(h)]).astype(BF16)
        sums.append(dot_nn(jnp.ones((8, TOK), BF16), kf)[0:1])
        for copy in range(4):
            s_ref[copy, head_cols(h), :] = state
    rows = sum_rows(sums)
    for copy in range(4):
        s_ref[copy, SUMS:ROWS, :] = rows


def total_kernel(r_ref, s_ref):
    total = r_ref[0].astype(F32)
    for j in range(1, 4):
        total = total + r_ref[j].astype(F32)
    state = total[:SUMS].astype(BF16)
    tail = total[SUMS:]
    rows = sum_rows([tail[h : h + 1] + tail[HEADS + h : HEADS + h + 1] for h in range(HEADS)])
    for copy in range(4):
        s_ref[copy, :SUMS, :] = state
        s_ref[copy, SUMS:ROWS, :] = rows


def table_parts(tab):
    hi = tab.astype(BF16)
    rest = tab - hi.astype(F32)
    mid = rest.astype(BF16)
    low = (rest - mid.astype(F32)).astype(BF16)
    return jnp.concatenate([hi, mid, low], axis=0)


def tile_weights(cls_row, tab3):
    hot = lax.broadcasted_iota(jnp.int32, (NCLASS, TILE), 0) == cls_row
    hot = jnp.where(hot, 1.0, 0.0).astype(BF16)
    return dot_tn(jnp.concatenate([hot, hot, hot], axis=0), tab3)


def local_kernel(q_ref, k_ref, v_ref, cls_ref, tab_ref, part_ref):
    t_row = lax.broadcasted_iota(jnp.int32, (TILE, TILE), 0)
    s_col = lax.broadcasted_iota(jnp.int32, (TILE, TILE), 1)
    same = (t_row // 64) == (s_col // 64)
    mask0 = same & (s_col <= t_row)
    mask1 = (t_row >= 64) & (s_col < 64)
    lane = s_col
    row_id = t_row
    tiles = TOK // TILE
    for h in range(HEADS):
        cols = head_cols(h)
        tab3 = table_parts(tab_ref[h])
        kf = [feats(k_ref[i * TILE : (i + 1) * TILE, cols]) for i in range(tiles)]
        vt = [v_ref[i * TILE : (i + 1) * TILE, cols] for i in range(tiles)]
        state = [dot_tn(kf[i], vt[i]) for i in range(tiles - 1)]
        ksum = [jnp.sum(kf[i].astype(F32), axis=0, keepdims=True) for i in range(tiles - 1)]
        group = {}
        for level, size in ((2, 1), (3, 2), (4, 4)):
            for first in range(0, tiles, 2 * size):
                st = state[first]
                ks = ksum[first]
                for other in range(first + 1, first + size):
                    st = st + state[other]
                    ks = ks + ksum[other]
                group[level, first] = (jnp.concatenate(hi_lo(st), axis=0), ks)
        for i in range(tiles):
            rows = slice(i * TILE, (i + 1) * TILE)
            qf = feats(q_ref[rows, cols])
            qq = jnp.concatenate([qf, qf], axis=1)
            sc = dot_nt(qf, kf[i])
            s0 = jnp.where(mask0, sc, 0.0)
            s1 = jnp.where(mask1, sc, 0.0)
            den = jnp.where(lane == 0, jnp.sum(s0, axis=1, keepdims=True), 0.0)
            den = jnp.where(lane == 1, jnp.sum(s1, axis=1, keepdims=True), den)
            far = []
            for level, size in ((2, 1), (3, 2), (4, 4)):
                if i & size:
                    far.append((level, group[level, i // (2 * size) * 2 * size]))
            if far:
                ks = jnp.zeros((TILE, E), F32)
                for level, (_, row) in far:
                    ks = jnp.where(row_id == level, row, ks)
                den = den + dot_nt(qq, jnp.concatenate(hi_lo(ks), axis=1))
            coeff = tile_weights(cls_ref[i : i + 1, :], tab3) / jnp.maximum(den, 1.0)
            weight = coeff[:, 0:1] * s0 + coeff[:, 1:2] * s1
            acc = dot_nn(weight.astype(BF16), vt[i])
            for level, (st, _) in far:
                acc = acc + coeff[:, level : level + 1] * dot_nn(qq, st)
            part_ref[rows, cols] = acc


def two_levels(axis, first_lane, r_ref, q_ref, cls_ref, tab_ref, part_ref, emit):
    me = lax.axis_index(axis)
    bit0 = (me & 1).astype(F32)
    bit1 = (me >> 1).astype(F32)
    near = r_ref[jnp.maximum(me - 1, 0)].astype(F32) * bit0
    wide = (r_ref[0].astype(F32) + r_ref[1].astype(F32)) * bit1
    row_id = lax.broadcasted_iota(jnp.int32, (TILE, E), 0)
    for h in range(HEADS):
        cols = head_cols(h)
        tab3 = table_parts(tab_ref[h])
        near_hi, near_lo = hi_lo(near[cols])
        wide_hi, wide_lo = hi_lo(wide[cols])
        state = jnp.concatenate(
            [
                jnp.concatenate([near_hi, wide_hi], axis=1),
                jnp.concatenate([near_lo, wide_lo], axis=1),
            ],
            axis=0,
        )
        a, b = SUMS + h, SUMS + HEADS + h
        ks = jnp.where(row_id == first_lane, near[a : a + 1] + near[b : b + 1], 0.0)
        ks = jnp.where(row_id == first_lane + 1, wide[a : a + 1] + wide[b : b + 1], ks)
        ks = jnp.concatenate(hi_lo(ks), axis=1)
        for i in range(TOK // TILE):
            rows = slice(i * TILE, (i + 1) * TILE)
            qf = feats(q_ref[rows, cols])
            qq = jnp.concatenate([qf, qf], axis=1)
            den = dot_nt(qq, ks)
            through = dot_nn(qq, state)
            coeff = tile_weights(cls_ref[i : i + 1, :], tab3) / jnp.maximum(den, 1.0)
            acc = part_ref[rows, cols]
            acc = acc + coeff[:, first_lane : first_lane + 1] * through[:, :E]
            acc = acc + coeff[:, first_lane + 1 : first_lane + 2] * through[:, E:]
            emit(rows, cols, acc)


def level_kernel(axis, first_lane, r_ref, q_ref, cls_ref, tab_ref, part_ref, out_ref):
    def emit(rows, cols, acc):
        out_ref[rows, cols] = acc

    two_levels(axis, first_lane, r_ref, q_ref, cls_ref, tab_ref, part_ref, emit)


def final_kernel(axis, first_lane, r_ref, q_ref, cls_ref, tab_ref, part_ref, mixed_ref, gated_ref):
    def emit(rows, cols, acc):
        mixed = acc.astype(BF16)
        mixed_ref[rows, cols] = mixed
        gate = 0.5 + 1.0 / (1.0 + jnp.exp(-mixed.astype(F32)))
        gated_ref[rows.start // TILE, :, cols] = (q_ref[rows, cols].astype(F32) * gate).astype(BF16)

    two_levels(axis, first_lane, r_ref, q_ref, cls_ref, tab_ref, part_ref, emit)


def window_kernel(xq_ref, k_ref, v_ref, seg_ref, rim1_ref, rim2_ref, out_ref):
    place = (
        (lax.axis_index("x") * 4 + lax.axis_index("zh")) * 4 + lax.axis_index("zl")
    ) * 8 + lax.axis_index("head")
    seg_own = seg_ref[0:1, :].astype(F32)
    seg_q = jnp.transpose(jnp.broadcast_to(seg_own, (TILE, TILE)))
    t_row = lax.broadcasted_iota(jnp.int32, (TILE, TILE), 0)
    s_col = lax.broadcasted_iota(jnp.int32, (TILE, TILE), 1)
    low = -1e30
    seg2 = rim2_ref[TILE : TILE + 1, :TILE].astype(F32)
    seg1 = rim1_ref[TILE : TILE + 1, :TILE].astype(F32)
    bias2 = jnp.where((seg_q == seg2) & (s_col > t_row) & (place >= 2), 0.0, low)
    bias1 = jnp.where((seg_q == seg1) & (place >= 1), 0.0, low)
    bias0 = jnp.where((seg_q == seg_own) & (s_col <= t_row), 0.0, low)
    bias = jnp.concatenate([bias2, bias1, bias0], axis=1)
    scale = E ** (-0.5) * LOG2E
    ones = jnp.ones((3 * TILE, E), BF16)
    for g in range(KVH):
        cols = slice(g * E, (g + 1) * E)
        vcols = slice((KVH + g) * E, (KVH + g + 1) * E)
        keys = jnp.concatenate([rim2_ref[:TILE, cols], rim1_ref[:TILE, cols], k_ref[:, cols]], axis=0)
        vals = jnp.concatenate([rim2_ref[:TILE, vcols], rim1_ref[:TILE, vcols], v_ref[:, cols]], axis=0)
        vals = jnp.concatenate([vals, ones], axis=1)
        for j in range(H // KVH):
            src, part = 2 * g + j // 2, j % 2
            sc = dot_nt(xq_ref[src, :, head_cols(part)], keys) * scale + bias
            top = jnp.max(sc, axis=1, keepdims=True)
            probs = jnp.exp2(sc - top).astype(BF16)
            res = dot_nn(probs, vals)
            head = g * (H // KVH) + j
            out_ref[:, head_cols(head)] = (res[:, :E] / res[:, E:]).astype(BF16)


def call(kernel, out, *args, aliases=None):
    return pl.pallas_call(
        kernel,
        out_shape=out,
        input_output_aliases=aliases or {},
        compiler_params=pltpu.CompilerParams(vmem_limit_bytes=40 * 1024 * 1024),
    )(*args)


def swap(value, axis):
    return lax.all_to_all(value, axis, split_axis=0, concat_axis=0, tiled=True)


def local(queries, lin_keys, lin_values, level_class, level_table, win_keys, win_values, seg_ids):
    sds = jax.ShapeDtypeStruct
    levels = level_table.shape[2]
    copies = sds((4, ROWS, E), BF16)
    part_shape = sds((TOK, HEADS * E), F32)
    own = call(state_kernel, copies, lin_keys, lin_values)
    from_zl = swap(own, "zl")
    cls = level_class.reshape(TOK // TILE, TILE)
    tab = jnp.pad(jnp.transpose(level_table, (1, 0, 2)), ((0, 0), (0, 0), (0, E - levels)))
    part = call(local_kernel, part_shape, queries, lin_keys, lin_values, cls, tab)
    from_zh = swap(call(total_kernel, copies, from_zl), "zh")
    seg_row = jnp.pad(seg_ids.astype(BF16)[None], ((0, 15), (0, 2 * KVH * E - TILE)))
    packed = jnp.concatenate([jnp.concatenate([win_keys, win_values], axis=1), seg_row], axis=0)
    flat = ("x", "zh", "zl", "head")
    rims = [lax.ppermute(packed, flat, [(i, i + d) for i in range(512 - d)]) for d in (1, 2)]
    part = call(
        functools.partial(level_kernel, "zl", 5), part_shape, from_zl, queries, cls, tab, part, aliases={4: 0}
    )
    from_x = swap(call(total_kernel, copies, from_zh), "x")
    part = call(
        functools.partial(level_kernel, "zh", 7), part_shape, from_zh, queries, cls, tab, part, aliases={4: 0}
    )
    mixed, gated = call(
        functools.partial(final_kernel, "x", 9),
        (sds((TOK, HEADS * E), BF16), sds((8, TILE, HEADS * E), BF16)),
        from_x,
        queries,
        cls,
        tab,
        part,
    )
    token_q = swap(gated, "head")
    out = call(
        window_kernel,
        sds((TILE, H * E), BF16),
        token_q,
        win_keys,
        win_values,
        jnp.broadcast_to(seg_ids[None], (8, TILE)),
        rims[0],
        rims[1],
    )
    return mixed, out


def solution(mesh):
    grid = Mesh(mesh.devices.reshape(4, 4, 4, 8), ("x", "zh", "zl", "head"))
    ctx = ("x", "zh", "zl")
    both = ("x", "zh", "zl", "head")
    return jax.shard_map(
        local,
        mesh=grid,
        in_specs=(
            P(ctx, "head"),
            P(ctx, "head"),
            P(ctx, "head"),
            P(ctx),
            P(None, "head", None),
            P(both, None),
            P(both, None),
            P(both),
        ),
        out_specs=(P(ctx, "head"), P(both, None)),
        check_vma=False,
    )
```

```python
import functools

import jax
import jax.numpy as jnp
from jax import lax
from jax.experimental import pallas as pl
from jax.experimental.pallas import tpu as pltpu
from jax.sharding import Mesh
from jax.sharding import PartitionSpec as P

H = 16
E = 128
KVH = 4
NCLASS = 16
HEADS = 2
TOK = 1024
TILE = 128
CHUNK = 256
CHUNKS = TOK // CHUNK
SUMS = HEADS * E
ROWS = SUMS + 16
F32 = jnp.float32
BF16 = jnp.bfloat16
LOG2E = 1.4426950408889634


def feats(x):
    x = x.astype(F32)
    return jnp.where(x > 0, x + 1.0, jnp.exp(x)).astype(BF16)


def dot_nn(a, b):
    return lax.dot_general(a, b, (((1,), (0,)), ((), ())), preferred_element_type=F32)


def dot_nt(a, b):
    return lax.dot_general(a, b, (((1,), (1,)), ((), ())), preferred_element_type=F32)


def dot_tn(a, b):
    return lax.dot_general(a, b, (((0,), (0,)), ((), ())), preferred_element_type=F32)


def hi_lo(x):
    hi = x.astype(BF16)
    return hi, (x - hi.astype(F32)).astype(BF16)


def head_cols(h):
    return slice(h * E, (h + 1) * E)


def sum_rows(sums):
    row = lax.broadcasted_iota(jnp.int32, (16, E), 0)
    out = jnp.zeros((16, E), F32)
    for h in range(HEADS):
        hi = sums[h].astype(BF16).astype(F32)
        out = jnp.where(row == h, hi, out)
        out = jnp.where(row == HEADS + h, sums[h] - hi, out)
    return out.astype(BF16)


def state_kernel(k_hbm, v_hbm, s_ref, k_ref, v_ref, sems):
    copies = []
    for i in range(CHUNKS):
        rows = slice(i * CHUNK, (i + 1) * CHUNK)
        pair = [
            pltpu.make_async_copy(src.at[rows], dst.at[rows], sems.at[n, i])
            for n, (src, dst) in enumerate(((k_hbm, k_ref), (v_hbm, v_ref)))
        ]
        for copy in pair:
            copy.start()
        copies.append(pair)
    state = [jnp.zeros((E, E), F32) for _ in range(HEADS)]
    sums = [jnp.zeros((8, E), F32) for _ in range(HEADS)]
    for i in range(CHUNKS):
        rows = slice(i * CHUNK, (i + 1) * CHUNK)
        for copy in copies[i]:
            copy.wait()
        for h in range(HEADS):
            kf = feats(k_ref[rows, head_cols(h)])
            state[h] = state[h] + dot_tn(kf, v_ref[rows, head_cols(h)])
            sums[h] = sums[h] + dot_nn(jnp.ones((8, CHUNK), BF16), kf)
    rows = sum_rows([sums[h][0:1] for h in range(HEADS)])
    for copy in range(4):
        for h in range(HEADS):
            s_ref[copy, head_cols(h), :] = state[h].astype(BF16)
        s_ref[copy, SUMS:ROWS, :] = rows


def total_kernel(r_ref, s_ref):
    total = r_ref[0].astype(F32)
    for j in range(1, 4):
        total = total + r_ref[j].astype(F32)
    state = total[:SUMS].astype(BF16)
    tail = total[SUMS:]
    rows = sum_rows([tail[h : h + 1] + tail[HEADS + h : HEADS + h + 1] for h in range(HEADS)])
    for copy in range(4):
        s_ref[copy, :SUMS, :] = state
        s_ref[copy, SUMS:ROWS, :] = rows


def table_parts(tab):
    hi = tab.astype(BF16)
    rest = tab - hi.astype(F32)
    mid = rest.astype(BF16)
    low = (rest - mid.astype(F32)).astype(BF16)
    return jnp.concatenate([hi, mid, low], axis=0)


def tile_weights(cls_row, tab3):
    hot = lax.broadcasted_iota(jnp.int32, (NCLASS, TILE), 0) == cls_row
    hot = jnp.where(hot, 1.0, 0.0).astype(BF16)
    return dot_tn(jnp.concatenate([hot, hot, hot], axis=0), tab3)


def local_kernel(q_ref, k_ref, v_ref, cls_ref, tab_ref, part_ref):
    t_row = lax.broadcasted_iota(jnp.int32, (TILE, TILE), 0)
    s_col = lax.broadcasted_iota(jnp.int32, (TILE, TILE), 1)
    same = (t_row // 64) == (s_col // 64)
    mask0 = same & (s_col <= t_row)
    mask1 = (t_row >= 64) & (s_col < 64)
    lane = s_col
    row_id = t_row
    tiles = TOK // TILE
    for h in range(HEADS):
        cols = head_cols(h)
        tab3 = table_parts(tab_ref[h])
        kf = [feats(k_ref[i * TILE : (i + 1) * TILE, cols]) for i in range(tiles)]
        vt = [v_ref[i * TILE : (i + 1) * TILE, cols] for i in range(tiles)]
        state = [dot_tn(kf[i], vt[i]) for i in range(tiles - 1)]
        ksum = [jnp.sum(kf[i].astype(F32), axis=0, keepdims=True) for i in range(tiles - 1)]
        group = {}
        for level, size in ((2, 1), (3, 2), (4, 4)):
            for first in range(0, tiles, 2 * size):
                st = state[first]
                ks = ksum[first]
                for other in range(first + 1, first + size):
                    st = st + state[other]
                    ks = ks + ksum[other]
                group[level, first] = (jnp.concatenate(hi_lo(st), axis=0), ks)
        for i in range(tiles):
            rows = slice(i * TILE, (i + 1) * TILE)
            qf = feats(q_ref[rows, cols])
            qq = jnp.concatenate([qf, qf], axis=1)
            sc = dot_nt(qf, kf[i])
            s0 = jnp.where(mask0, sc, 0.0)
            s1 = jnp.where(mask1, sc, 0.0)
            den = jnp.where(lane == 0, jnp.sum(s0, axis=1, keepdims=True), 0.0)
            den = jnp.where(lane == 1, jnp.sum(s1, axis=1, keepdims=True), den)
            far = []
            for level, size in ((2, 1), (3, 2), (4, 4)):
                if i & size:
                    far.append((level, group[level, i // (2 * size) * 2 * size]))
            if far:
                ks = jnp.zeros((TILE, E), F32)
                for level, (_, row) in far:
                    ks = jnp.where(row_id == level, row, ks)
                den = den + dot_nt(qq, jnp.concatenate(hi_lo(ks), axis=1))
            coeff = tile_weights(cls_ref[i : i + 1, :], tab3) / jnp.maximum(den, 1.0)
            weight = coeff[:, 0:1] * s0 + coeff[:, 1:2] * s1
            acc = dot_nn(weight.astype(BF16), vt[i])
            for level, (st, _) in far:
                acc = acc + coeff[:, level : level + 1] * dot_nn(qq, st)
            part_ref[rows, cols] = acc


def two_levels(axis, first_lane, r_ref, q_ref, cls_ref, tab_ref, part_ref, emit):
    me = lax.axis_index(axis)
    bit0 = (me & 1).astype(F32)
    bit1 = (me >> 1).astype(F32)
    near = r_ref[jnp.maximum(me - 1, 0)].astype(F32) * bit0
    wide = (r_ref[0].astype(F32) + r_ref[1].astype(F32)) * bit1
    row_id = lax.broadcasted_iota(jnp.int32, (TILE, E), 0)
    for h in range(HEADS):
        cols = head_cols(h)
        tab3 = table_parts(tab_ref[h])
        near_hi, near_lo = hi_lo(near[cols])
        wide_hi, wide_lo = hi_lo(wide[cols])
        state = jnp.concatenate(
            [
                jnp.concatenate([near_hi, wide_hi], axis=1),
                jnp.concatenate([near_lo, wide_lo], axis=1),
            ],
            axis=0,
        )
        a, b = SUMS + h, SUMS + HEADS + h
        ks = jnp.where(row_id == first_lane, near[a : a + 1] + near[b : b + 1], 0.0)
        ks = jnp.where(row_id == first_lane + 1, wide[a : a + 1] + wide[b : b + 1], ks)
        ks = jnp.concatenate(hi_lo(ks), axis=1)
        for i in range(TOK // TILE):
            rows = slice(i * TILE, (i + 1) * TILE)
            qf = feats(q_ref[rows, cols])
            qq = jnp.concatenate([qf, qf], axis=1)
            den = dot_nt(qq, ks)
            through = dot_nn(qq, state)
            coeff = tile_weights(cls_ref[i : i + 1, :], tab3) / jnp.maximum(den, 1.0)
            acc = part_ref[rows, cols]
            acc = acc + coeff[:, first_lane : first_lane + 1] * through[:, :E]
            acc = acc + coeff[:, first_lane + 1 : first_lane + 2] * through[:, E:]
            emit(rows, cols, acc)


def level_kernel(axis, first_lane, r_ref, q_ref, cls_ref, tab_ref, part_ref, out_ref):
    def emit(rows, cols, acc):
        out_ref[rows, cols] = acc

    two_levels(axis, first_lane, r_ref, q_ref, cls_ref, tab_ref, part_ref, emit)


def final_kernel(axis, first_lane, r_ref, q_ref, cls_ref, tab_ref, part_ref, mixed_ref, gated_ref):
    def emit(rows, cols, acc):
        mixed = acc.astype(BF16)
        mixed_ref[rows, cols] = mixed
        gate = 0.5 + 1.0 / (1.0 + jnp.exp(-mixed.astype(F32)))
        gated_ref[rows.start // TILE, :, cols] = (q_ref[rows, cols].astype(F32) * gate).astype(BF16)

    two_levels(axis, first_lane, r_ref, q_ref, cls_ref, tab_ref, part_ref, emit)


def window_kernel(xq_ref, k_ref, v_ref, seg_ref, rim1_ref, rim2_ref, out_ref):
    place = (
        (lax.axis_index("x") * 4 + lax.axis_index("zh")) * 4 + lax.axis_index("zl")
    ) * 8 + lax.axis_index("head")
    seg_own = seg_ref[0:1, :].astype(F32)
    seg_q = jnp.transpose(jnp.broadcast_to(seg_own, (TILE, TILE)))
    t_row = lax.broadcasted_iota(jnp.int32, (TILE, TILE), 0)
    s_col = lax.broadcasted_iota(jnp.int32, (TILE, TILE), 1)
    low = -1e30
    seg2 = rim2_ref[TILE : TILE + 1, :TILE].astype(F32)
    seg1 = rim1_ref[TILE : TILE + 1, :TILE].astype(F32)
    bias2 = jnp.where((seg_q == seg2) & (s_col > t_row) & (place >= 2), 0.0, low)
    bias1 = jnp.where((seg_q == seg1) & (place >= 1), 0.0, low)
    bias0 = jnp.where((seg_q == seg_own) & (s_col <= t_row), 0.0, low)
    bias = jnp.concatenate([bias2, bias1, bias0], axis=1)
    scale = E ** (-0.5) * LOG2E
    ones = jnp.ones((3 * TILE, E), BF16)
    for g in range(KVH):
        cols = slice(g * E, (g + 1) * E)
        vcols = slice((KVH + g) * E, (KVH + g + 1) * E)
        keys = jnp.concatenate([rim2_ref[:TILE, cols], rim1_ref[:TILE, cols], k_ref[:, cols]], axis=0)
        vals = jnp.concatenate([rim2_ref[:TILE, vcols], rim1_ref[:TILE, vcols], v_ref[:, cols]], axis=0)
        vals = jnp.concatenate([vals, ones], axis=1)
        for j in range(H // KVH):
            src, part = 2 * g + j // 2, j % 2
            sc = dot_nt(xq_ref[src, :, head_cols(part)], keys) * scale + bias
            top = jnp.max(sc, axis=1, keepdims=True)
            probs = jnp.exp2(sc - top).astype(BF16)
            res = dot_nn(probs, vals)
            head = g * (H // KVH) + j
            out_ref[:, head_cols(head)] = (res[:, :E] / res[:, E:]).astype(BF16)


def call(kernel, out, *args, after=(), aliases=None):
    count = len(args)

    def body(*refs):
        kernel(*refs[:count], *refs[count + len(after) :])

    vmem = pl.BlockSpec(memory_space=pltpu.VMEM)
    return pl.pallas_call(
        body,
        out_shape=out,
        in_specs=[vmem] * count + [pl.BlockSpec(memory_space=pl.ANY)] * len(after),
        input_output_aliases=aliases or {},
        compiler_params=pltpu.CompilerParams(vmem_limit_bytes=32 * 1024 * 1024),
    )(*args, *after)


def span_state(keys, values):
    hbm = pl.BlockSpec(memory_space=pltpu.HBM)
    return pl.pallas_call(
        state_kernel,
        out_shape=jax.ShapeDtypeStruct((4, ROWS, E), BF16),
        in_specs=[hbm, hbm],
        scratch_shapes=[
            pltpu.VMEM((TOK, HEADS * E), BF16),
            pltpu.VMEM((TOK, HEADS * E), BF16),
            pltpu.SemaphoreType.DMA((2, CHUNKS)),
        ],
        compiler_params=pltpu.CompilerParams(vmem_limit_bytes=60 * 1024 * 1024),
    )(keys, values)


def pack_kernel(k_ref, v_ref, seg_ref, out_ref):
    width = KVH * E
    out_ref[:TILE, :width] = k_ref[...]
    out_ref[:TILE, width:] = v_ref[...]
    out_ref[TILE:, :] = jnp.zeros((16, 2 * width), BF16)
    out_ref[TILE:, :TILE] = jnp.broadcast_to(seg_ref[0:1, :].astype(F32), (16, TILE)).astype(BF16)


def swap(value, axis):
    return lax.all_to_all(value, axis, split_axis=0, concat_axis=0, tiled=True)


def local(queries, lin_keys, lin_values, level_class, level_table, win_keys, win_values, seg_ids):
    sds = jax.ShapeDtypeStruct
    levels = level_table.shape[2]
    copies = sds((4, ROWS, E), BF16)
    part_shape = sds((TOK, HEADS * E), F32)
    cls = level_class.reshape(TOK // TILE, TILE)
    tab = jnp.pad(jnp.transpose(level_table, (1, 0, 2)), ((0, 0), (0, 0), (0, E - levels)))
    seg_rows = jnp.broadcast_to(seg_ids[None], (8, TILE))

    sum1 = span_state(lin_keys, lin_values)
    from_zl = swap(sum1, "zl")
    part = call(local_kernel, part_shape, queries, lin_keys, lin_values, cls, tab, after=(sum1,))

    sum4 = call(total_kernel, copies, from_zl, after=(part,))
    from_zh = swap(sum4, "zh")
    packed = call(pack_kernel, sds((TILE + 16, 2 * KVH * E), BF16), win_keys, win_values, seg_rows, after=(sum4,))
    flat = ("x", "zh", "zl", "head")
    rims = [lax.ppermute(packed, flat, [(i, i + d) for i in range(512 - d)]) for d in (1, 2)]
    part = call(
        functools.partial(level_kernel, "zl", 5),
        part_shape,
        from_zl,
        queries,
        cls,
        tab,
        part,
        after=(packed,),
        aliases={4: 0},
    )

    sum16 = call(total_kernel, copies, from_zh, after=(part, rims[0], rims[1]))
    from_x = swap(sum16, "x")
    part = call(
        functools.partial(level_kernel, "zh", 7),
        part_shape,
        from_zh,
        queries,
        cls,
        tab,
        part,
        after=(sum16,),
        aliases={4: 0},
    )
    mixed, gated = call(
        functools.partial(final_kernel, "x", 9),
        (sds((TOK, HEADS * E), BF16), sds((8, TILE, HEADS * E), BF16)),
        from_x,
        queries,
        cls,
        tab,
        part,
    )
    token_q = swap(gated, "head")
    out = call(window_kernel, sds((TILE, H * E), BF16), token_q, win_keys, win_values, seg_rows, rims[0], rims[1])
    return mixed, out


def solution(mesh):
    grid = Mesh(mesh.devices.reshape(4, 4, 4, 8), ("x", "zh", "zl", "head"))
    ctx = ("x", "zh", "zl")
    both = ("x", "zh", "zl", "head")
    return jax.shard_map(
        local,
        mesh=grid,
        in_specs=(
            P(ctx, "head"),
            P(ctx, "head"),
            P(ctx, "head"),
            P(ctx),
            P(None, "head", None),
            P(both, None),
            P(both, None),
            P(both),
        ),
        out_specs=(P(ctx, "head"), P(both, None)),
        check_vma=False,
    )
```

```python
import functools

import jax
import jax.numpy as jnp
from jax import lax
from jax.experimental import pallas as pl
from jax.experimental.pallas import tpu as pltpu
from jax.sharding import Mesh
from jax.sharding import PartitionSpec as P

H = 16
E = 128
KVH = 4
NCLASS = 16
HEADS = 2
TOK = 1024
TILE = 128
CHUNK = 512
CHUNKS = TOK // CHUNK
SUMS = HEADS * E
ROWS = SUMS + 16
F32 = jnp.float32
BF16 = jnp.bfloat16
LOG2E = 1.4426950408889634


def feats(x):
    x = x.astype(F32)
    return jnp.where(x > 0, x + 1.0, jnp.exp(x)).astype(BF16)


def dot_nn(a, b):
    return lax.dot_general(a, b, (((1,), (0,)), ((), ())), preferred_element_type=F32)


def dot_nt(a, b):
    return lax.dot_general(a, b, (((1,), (1,)), ((), ())), preferred_element_type=F32)


def dot_tn(a, b):
    return lax.dot_general(a, b, (((0,), (0,)), ((), ())), preferred_element_type=F32)


def hi_lo(x):
    hi = x.astype(BF16)
    return hi, (x - hi.astype(F32)).astype(BF16)


def head_cols(h):
    return slice(h * E, (h + 1) * E)


def sum_rows(sums):
    row = lax.broadcasted_iota(jnp.int32, (16, E), 0)
    out = jnp.zeros((16, E), F32)
    for h in range(HEADS):
        hi = sums[h].astype(BF16).astype(F32)
        out = jnp.where(row == h, hi, out)
        out = jnp.where(row == HEADS + h, sums[h] - hi, out)
    return out.astype(BF16)


def state_kernel(k_hbm, v_hbm, s_ref, k_ref, v_ref, sems):
    copies = []
    for i in range(CHUNKS):
        rows = slice(i * CHUNK, (i + 1) * CHUNK)
        pair = [
            pltpu.make_async_copy(src.at[rows], dst.at[rows], sems.at[n, i])
            for n, (src, dst) in enumerate(((k_hbm, k_ref), (v_hbm, v_ref)))
        ]
        for copy in pair:
            copy.start()
        copies.append(pair)
    state = [jnp.zeros((E, E), F32) for _ in range(HEADS)]
    sums = [jnp.zeros((8, E), F32) for _ in range(HEADS)]
    for i in range(CHUNKS):
        rows = slice(i * CHUNK, (i + 1) * CHUNK)
        for copy in copies[i]:
            copy.wait()
        for h in range(HEADS):
            kf = feats(k_ref[rows, head_cols(h)])
            state[h] = state[h] + dot_tn(kf, v_ref[rows, head_cols(h)])
            sums[h] = sums[h] + dot_nn(jnp.ones((8, CHUNK), BF16), kf)
    rows = sum_rows([sums[h][0:1] for h in range(HEADS)])
    for copy in range(4):
        for h in range(HEADS):
            s_ref[copy, head_cols(h), :] = state[h].astype(BF16)
        s_ref[copy, SUMS:ROWS, :] = rows


def total_kernel(r_ref, s_ref):
    total = r_ref[0].astype(F32)
    for j in range(1, 4):
        total = total + r_ref[j].astype(F32)
    state = total[:SUMS].astype(BF16)
    tail = total[SUMS:]
    rows = sum_rows([tail[h : h + 1] + tail[HEADS + h : HEADS + h + 1] for h in range(HEADS)])
    for copy in range(4):
        s_ref[copy, :SUMS, :] = state
        s_ref[copy, SUMS:ROWS, :] = rows


def table_parts(tab):
    hi = tab.astype(BF16)
    rest = tab - hi.astype(F32)
    mid = rest.astype(BF16)
    low = (rest - mid.astype(F32)).astype(BF16)
    return jnp.concatenate([hi, mid, low], axis=0)


def tile_weights(cls_row, tab3):
    hot = lax.broadcasted_iota(jnp.int32, (NCLASS, TILE), 0) == cls_row
    hot = jnp.where(hot, 1.0, 0.0).astype(BF16)
    return dot_tn(jnp.concatenate([hot, hot, hot], axis=0), tab3)


def local_kernel(q_ref, k_ref, v_ref, cls_ref, tab_ref, part_ref):
    t_row = lax.broadcasted_iota(jnp.int32, (TILE, TILE), 0)
    s_col = lax.broadcasted_iota(jnp.int32, (TILE, TILE), 1)
    same = (t_row // 64) == (s_col // 64)
    mask0 = same & (s_col <= t_row)
    mask1 = (t_row >= 64) & (s_col < 64)
    lane = s_col
    row_id = t_row
    tiles = TOK // TILE
    for h in range(HEADS):
        cols = head_cols(h)
        tab3 = table_parts(tab_ref[h])
        kf = [feats(k_ref[i * TILE : (i + 1) * TILE, cols]) for i in range(tiles)]
        vt = [v_ref[i * TILE : (i + 1) * TILE, cols] for i in range(tiles)]
        state = [dot_tn(kf[i], vt[i]) for i in range(tiles - 1)]
        ksum = [jnp.sum(kf[i].astype(F32), axis=0, keepdims=True) for i in range(tiles - 1)]
        group = {}
        for level, size in ((2, 1), (3, 2), (4, 4)):
            for first in range(0, tiles, 2 * size):
                st = state[first]
                ks = ksum[first]
                for other in range(first + 1, first + size):
                    st = st + state[other]
                    ks = ks + ksum[other]
                group[level, first] = (jnp.concatenate(hi_lo(st), axis=0), ks)
        for i in range(tiles):
            rows = slice(i * TILE, (i + 1) * TILE)
            qf = feats(q_ref[rows, cols])
            qq = jnp.concatenate([qf, qf], axis=1)
            sc = dot_nt(qf, kf[i])
            s0 = jnp.where(mask0, sc, 0.0)
            s1 = jnp.where(mask1, sc, 0.0)
            den = jnp.where(lane == 0, jnp.sum(s0, axis=1, keepdims=True), 0.0)
            den = jnp.where(lane == 1, jnp.sum(s1, axis=1, keepdims=True), den)
            far = []
            for level, size in ((2, 1), (3, 2), (4, 4)):
                if i & size:
                    far.append((level, group[level, i // (2 * size) * 2 * size]))
            if far:
                ks = jnp.zeros((TILE, E), F32)
                for level, (_, row) in far:
                    ks = jnp.where(row_id == level, row, ks)
                den = den + dot_nt(qq, jnp.concatenate(hi_lo(ks), axis=1))
            coeff = tile_weights(cls_ref[i : i + 1, :], tab3) / jnp.maximum(den, 1.0)
            weight = coeff[:, 0:1] * s0 + coeff[:, 1:2] * s1
            acc = dot_nn(weight.astype(BF16), vt[i])
            for level, (st, _) in far:
                acc = acc + coeff[:, level : level + 1] * dot_nn(qq, st)
            part_ref[rows, cols] = acc


def two_levels(axis, first_lane, r_ref, q_ref, cls_ref, tab_ref, part_ref, emit):
    me = lax.axis_index(axis)
    bit0 = (me & 1).astype(F32)
    bit1 = (me >> 1).astype(F32)
    near = r_ref[jnp.maximum(me - 1, 0)].astype(F32) * bit0
    wide = (r_ref[0].astype(F32) + r_ref[1].astype(F32)) * bit1
    row_id = lax.broadcasted_iota(jnp.int32, (TILE, E), 0)
    for h in range(HEADS):
        cols = head_cols(h)
        tab3 = table_parts(tab_ref[h])
        near_hi, near_lo = hi_lo(near[cols])
        wide_hi, wide_lo = hi_lo(wide[cols])
        state = jnp.concatenate(
            [
                jnp.concatenate([near_hi, wide_hi], axis=1),
                jnp.concatenate([near_lo, wide_lo], axis=1),
            ],
            axis=0,
        )
        a, b = SUMS + h, SUMS + HEADS + h
        ks = jnp.where(row_id == first_lane, near[a : a + 1] + near[b : b + 1], 0.0)
        ks = jnp.where(row_id == first_lane + 1, wide[a : a + 1] + wide[b : b + 1], ks)
        ks = jnp.concatenate(hi_lo(ks), axis=1)
        for i in range(TOK // TILE):
            rows = slice(i * TILE, (i + 1) * TILE)
            qf = feats(q_ref[rows, cols])
            qq = jnp.concatenate([qf, qf], axis=1)
            den = dot_nt(qq, ks)
            through = dot_nn(qq, state)
            coeff = tile_weights(cls_ref[i : i + 1, :], tab3) / jnp.maximum(den, 1.0)
            acc = part_ref[rows, cols]
            acc = acc + coeff[:, first_lane : first_lane + 1] * through[:, :E]
            acc = acc + coeff[:, first_lane + 1 : first_lane + 2] * through[:, E:]
            emit(rows, cols, acc)


def level_kernel(axis, first_lane, r_ref, q_ref, cls_ref, tab_ref, part_ref, out_ref):
    def emit(rows, cols, acc):
        out_ref[rows, cols] = acc

    two_levels(axis, first_lane, r_ref, q_ref, cls_ref, tab_ref, part_ref, emit)


def final_kernel(axis, first_lane, r_ref, q_ref, cls_ref, tab_ref, part_ref, mixed_ref, gated_ref):
    def emit(rows, cols, acc):
        mixed = acc.astype(BF16)
        mixed_ref[rows, cols] = mixed
        gate = 0.5 + 1.0 / (1.0 + jnp.exp(-mixed.astype(F32)))
        gated_ref[rows.start // TILE, :, cols] = (q_ref[rows, cols].astype(F32) * gate).astype(BF16)

    two_levels(axis, first_lane, r_ref, q_ref, cls_ref, tab_ref, part_ref, emit)


def window_kernel(xq_ref, k_ref, v_ref, seg_ref, rim1_ref, rim2_ref, out_ref):
    place = (
        (lax.axis_index("x") * 4 + lax.axis_index("zh")) * 4 + lax.axis_index("zl")
    ) * 8 + lax.axis_index("head")
    seg_own = seg_ref[0:1, :].astype(F32)
    seg_q = jnp.transpose(jnp.broadcast_to(seg_own, (TILE, TILE)))
    t_row = lax.broadcasted_iota(jnp.int32, (TILE, TILE), 0)
    s_col = lax.broadcasted_iota(jnp.int32, (TILE, TILE), 1)
    low = -1e30
    seg2 = rim2_ref[TILE : TILE + 1, :TILE].astype(F32)
    seg1 = rim1_ref[TILE : TILE + 1, :TILE].astype(F32)
    bias2 = jnp.where((seg_q == seg2) & (s_col > t_row) & (place >= 2), 0.0, low)
    bias1 = jnp.where((seg_q == seg1) & (place >= 1), 0.0, low)
    bias0 = jnp.where((seg_q == seg_own) & (s_col <= t_row), 0.0, low)
    bias = jnp.concatenate([bias2, bias1, bias0], axis=1)
    scale = E ** (-0.5) * LOG2E
    ones = jnp.ones((3 * TILE, E), BF16)
    for g in range(KVH):
        cols = slice(g * E, (g + 1) * E)
        vcols = slice((KVH + g) * E, (KVH + g + 1) * E)
        keys = jnp.concatenate([rim2_ref[:TILE, cols], rim1_ref[:TILE, cols], k_ref[:, cols]], axis=0)
        vals = jnp.concatenate([rim2_ref[:TILE, vcols], rim1_ref[:TILE, vcols], v_ref[:, cols]], axis=0)
        vals = jnp.concatenate([vals, ones], axis=1)
        for j in range(H // KVH):
            src, part = 2 * g + j // 2, j % 2
            sc = dot_nt(xq_ref[src, :, head_cols(part)], keys) * scale + bias
            top = jnp.max(sc, axis=1, keepdims=True)
            probs = jnp.exp2(sc - top).astype(BF16)
            res = dot_nn(probs, vals)
            head = g * (H // KVH) + j
            out_ref[:, head_cols(head)] = (res[:, :E] / res[:, E:]).astype(BF16)


def call(kernel, out, *args, after=(), aliases=None):
    count = len(args)

    def body(*refs):
        kernel(*refs[:count], *refs[count + len(after) :])

    vmem = pl.BlockSpec(memory_space=pltpu.VMEM)
    return pl.pallas_call(
        body,
        out_shape=out,
        in_specs=[vmem] * count + [pl.BlockSpec(memory_space=pl.ANY)] * len(after),
        input_output_aliases=aliases or {},
        compiler_params=pltpu.CompilerParams(vmem_limit_bytes=32 * 1024 * 1024),
    )(*args, *after)


def span_state(keys, values):
    hbm = pl.BlockSpec(memory_space=pltpu.HBM)
    return pl.pallas_call(
        state_kernel,
        out_shape=jax.ShapeDtypeStruct((4, ROWS, E), BF16),
        in_specs=[hbm, hbm],
        scratch_shapes=[
            pltpu.VMEM((TOK, HEADS * E), BF16),
            pltpu.VMEM((TOK, HEADS * E), BF16),
            pltpu.SemaphoreType.DMA((2, CHUNKS)),
        ],
        compiler_params=pltpu.CompilerParams(vmem_limit_bytes=60 * 1024 * 1024),
    )(keys, values)


def pack_kernel(k_ref, v_ref, seg_ref, out_ref):
    width = KVH * E
    out_ref[:TILE, :width] = k_ref[...]
    out_ref[:TILE, width:] = v_ref[...]
    out_ref[TILE:, :] = jnp.zeros((16, 2 * width), BF16)
    out_ref[TILE:, :TILE] = jnp.broadcast_to(seg_ref[0:1, :].astype(F32), (16, TILE)).astype(BF16)


def pick_kernel(own_ref, got_ref, out_ref):
    first = lax.rem(lax.axis_index("head"), 2) == 0

    @pl.when(first)
    def _():
        out_ref[...] = own_ref[...]

    @pl.when(jnp.logical_not(first))
    def _():
        out_ref[...] = got_ref[...]


def swap(value, axis):
    return lax.all_to_all(value, axis, split_axis=0, concat_axis=0, tiled=True)


def local(queries, lin_keys, lin_values, level_class, level_table, win_keys, win_values, seg_ids):
    sds = jax.ShapeDtypeStruct
    levels = level_table.shape[2]
    copies = sds((4, ROWS, E), BF16)
    part_shape = sds((TOK, HEADS * E), F32)
    cls = level_class.reshape(TOK // TILE, TILE)
    tab = jnp.pad(jnp.transpose(level_table, (1, 0, 2)), ((0, 0), (0, 0), (0, E - levels)))
    seg_rows = jnp.broadcast_to(seg_ids[None], (8, TILE))

    sum1 = span_state(lin_keys, lin_values)
    from_zl = swap(sum1, "zl")
    sum4 = call(total_kernel, copies, from_zl)
    from_zh = swap(sum4, "zh")
    part = call(local_kernel, part_shape, queries, lin_keys, lin_values, cls, tab, after=(sum4,))
    part = call(
        functools.partial(level_kernel, "zl", 5), part_shape, from_zl, queries, cls, tab, part, aliases={4: 0}
    )

    sum16 = call(total_kernel, copies, from_zh, after=(part,))
    from_x = swap(sum16, "x")
    rim = sds((TILE + 16, 2 * KVH * E), BF16)
    packed = call(pack_kernel, rim, win_keys, win_values, seg_rows, after=(sum16,))
    flat = ("x", "zh", "zl", "head")
    rim2 = lax.ppermute(packed, flat, [(i, i + 2) for i in range(510)])
    part = call(
        functools.partial(level_kernel, "zh", 7),
        part_shape,
        from_zh,
        queries,
        cls,
        tab,
        part,
        after=(packed,),
        aliases={4: 0},
    )
    mixed, gated = call(
        functools.partial(final_kernel, "x", 9),
        (sds((TOK, HEADS * E), BF16), sds((8, TILE, HEADS * E), BF16)),
        from_x,
        queries,
        cls,
        tab,
        part,
    )
    token_q = swap(gated, "head")
    picked = call(pick_kernel, rim, packed, rim2, after=(gated,))
    rim1 = lax.ppermute(picked, "head", [(i, i ^ 1) for i in range(8)])
    out = call(window_kernel, sds((TILE, H * E), BF16), token_q, win_keys, win_values, seg_rows, rim1, rim2)
    return mixed, out


def solution(mesh):
    grid = Mesh(mesh.devices.reshape(4, 4, 4, 8), ("x", "zh", "zl", "head"))
    ctx = ("x", "zh", "zl")
    both = ("x", "zh", "zl", "head")
    return jax.shard_map(
        local,
        mesh=grid,
        in_specs=(
            P(ctx, "head"),
            P(ctx, "head"),
            P(ctx, "head"),
            P(ctx),
            P(None, "head", None),
            P(both, None),
            P(both, None),
            P(both),
        ),
        out_specs=(P(ctx, "head"), P(both, None)),
        check_vma=False,
    )
```

```python
import functools

import jax
import jax.numpy as jnp
from jax import lax
from jax.experimental import pallas as pl
from jax.experimental.pallas import tpu as pltpu
from jax.sharding import Mesh
from jax.sharding import PartitionSpec as P

H = 16
E = 128
KVH = 4
NCLASS = 16
HEADS = 2
TOK = 1024
TILE = 128
CHUNK = 512
PLAIN = (0, 1, 2, 3)
ZL_ORDER = (1, 2, 0, 3)
ZH_ORDER = (2, 0, 1, 3)
CHUNKS = TOK // CHUNK
SUMS = HEADS * E
ROWS = SUMS + 16
F32 = jnp.float32
BF16 = jnp.bfloat16
LOG2E = 1.4426950408889634


def feats(x):
    x = x.astype(F32)
    return jnp.where(x > 0, x + 1.0, jnp.exp(x)).astype(BF16)


def dot_nn(a, b):
    return lax.dot_general(a, b, (((1,), (0,)), ((), ())), preferred_element_type=F32)


def dot_nt(a, b):
    return lax.dot_general(a, b, (((1,), (1,)), ((), ())), preferred_element_type=F32)


def dot_tn(a, b):
    return lax.dot_general(a, b, (((0,), (0,)), ((), ())), preferred_element_type=F32)


def hi_lo(x):
    hi = x.astype(BF16)
    return hi, (x - hi.astype(F32)).astype(BF16)


def head_cols(h):
    return slice(h * E, (h + 1) * E)


def sum_rows(sums):
    row = lax.broadcasted_iota(jnp.int32, (16, E), 0)
    out = jnp.zeros((16, E), F32)
    for h in range(HEADS):
        hi = sums[h].astype(BF16).astype(F32)
        out = jnp.where(row == h, hi, out)
        out = jnp.where(row == HEADS + h, sums[h] - hi, out)
    return out.astype(BF16)


def state_kernel(k_hbm, v_hbm, s_ref, k_ref, v_ref, sems):
    copies = []
    for i in range(CHUNKS):
        rows = slice(i * CHUNK, (i + 1) * CHUNK)
        pair = [
            pltpu.make_async_copy(src.at[rows], dst.at[rows], sems.at[n, i])
            for n, (src, dst) in enumerate(((k_hbm, k_ref), (v_hbm, v_ref)))
        ]
        for copy in pair:
            copy.start()
        copies.append(pair)
    state = [jnp.zeros((E, E), F32) for _ in range(HEADS)]
    sums = [jnp.zeros((8, E), F32) for _ in range(HEADS)]
    for i in range(CHUNKS):
        rows = slice(i * CHUNK, (i + 1) * CHUNK)
        for copy in copies[i]:
            copy.wait()
        for h in range(HEADS):
            kf = feats(k_ref[rows, head_cols(h)])
            state[h] = state[h] + dot_tn(kf, v_ref[rows, head_cols(h)])
            sums[h] = sums[h] + dot_nn(jnp.ones((8, CHUNK), BF16), kf)
    rows = sum_rows([sums[h][0:1] for h in range(HEADS)])
    for copy in range(4):
        for h in range(HEADS):
            s_ref[copy, head_cols(h), :] = state[h].astype(BF16)
        s_ref[copy, SUMS:ROWS, :] = rows


def total_kernel(r_ref, s_ref):
    total = r_ref[0].astype(F32)
    for j in range(1, 4):
        total = total + r_ref[j].astype(F32)
    state = total[:SUMS].astype(BF16)
    tail = total[SUMS:]
    rows = sum_rows([tail[h : h + 1] + tail[HEADS + h : HEADS + h + 1] for h in range(HEADS)])
    for copy in range(4):
        s_ref[copy, :SUMS, :] = state
        s_ref[copy, SUMS:ROWS, :] = rows


def table_parts(tab):
    hi = tab.astype(BF16)
    rest = tab - hi.astype(F32)
    mid = rest.astype(BF16)
    low = (rest - mid.astype(F32)).astype(BF16)
    return jnp.concatenate([hi, mid, low], axis=0)


def tile_weights(cls_row, tab3):
    hot = lax.broadcasted_iota(jnp.int32, (NCLASS, TILE), 0) == cls_row
    hot = jnp.where(hot, 1.0, 0.0).astype(BF16)
    return dot_tn(jnp.concatenate([hot, hot, hot], axis=0), tab3)


def local_kernel(q_ref, k_ref, v_ref, cls_ref, tab_ref, part_ref):
    t_row = lax.broadcasted_iota(jnp.int32, (TILE, TILE), 0)
    s_col = lax.broadcasted_iota(jnp.int32, (TILE, TILE), 1)
    same = (t_row // 64) == (s_col // 64)
    mask0 = same & (s_col <= t_row)
    mask1 = (t_row >= 64) & (s_col < 64)
    lane = s_col
    row_id = t_row
    tiles = TOK // TILE
    for h in range(HEADS):
        cols = head_cols(h)
        tab3 = table_parts(tab_ref[h])
        kf = [feats(k_ref[i * TILE : (i + 1) * TILE, cols]) for i in range(tiles)]
        vt = [v_ref[i * TILE : (i + 1) * TILE, cols] for i in range(tiles)]
        state = [dot_tn(kf[i], vt[i]) for i in range(tiles - 1)]
        ksum = [jnp.sum(kf[i].astype(F32), axis=0, keepdims=True) for i in range(tiles - 1)]
        group = {}
        for level, size in ((2, 1), (3, 2), (4, 4)):
            for first in range(0, tiles, 2 * size):
                st = state[first]
                ks = ksum[first]
                for other in range(first + 1, first + size):
                    st = st + state[other]
                    ks = ks + ksum[other]
                group[level, first] = (jnp.concatenate(hi_lo(st), axis=0), ks)
        for i in range(tiles):
            rows = slice(i * TILE, (i + 1) * TILE)
            qf = feats(q_ref[rows, cols])
            qq = jnp.concatenate([qf, qf], axis=1)
            sc = dot_nt(qf, kf[i])
            s0 = jnp.where(mask0, sc, 0.0)
            s1 = jnp.where(mask1, sc, 0.0)
            den = jnp.where(lane == 0, jnp.sum(s0, axis=1, keepdims=True), 0.0)
            den = jnp.where(lane == 1, jnp.sum(s1, axis=1, keepdims=True), den)
            far = []
            for level, size in ((2, 1), (3, 2), (4, 4)):
                if i & size:
                    far.append((level, group[level, i // (2 * size) * 2 * size]))
            if far:
                ks = jnp.zeros((TILE, E), F32)
                for level, (_, row) in far:
                    ks = jnp.where(row_id == level, row, ks)
                den = den + dot_nt(qq, jnp.concatenate(hi_lo(ks), axis=1))
            coeff = tile_weights(cls_ref[i : i + 1, :], tab3) / jnp.maximum(den, 1.0)
            weight = coeff[:, 0:1] * s0 + coeff[:, 1:2] * s1
            acc = dot_nn(weight.astype(BF16), vt[i])
            for level, (st, _) in far:
                acc = acc + coeff[:, level : level + 1] * dot_nn(qq, st)
            part_ref[rows, cols] = acc


def two_levels(axis, order, first_lane, r_ref, q_ref, cls_ref, tab_ref, part_ref, emit):
    me = lax.axis_index(axis)
    bit0 = (me & 1).astype(F32)
    bit1 = (me >> 1).astype(F32)
    place = [order.index(j) for j in range(4)]
    neighbour = jnp.where(me == 3, place[2], place[0])
    near = r_ref[neighbour].astype(F32) * bit0
    wide = (r_ref[place[0]].astype(F32) + r_ref[place[1]].astype(F32)) * bit1
    row_id = lax.broadcasted_iota(jnp.int32, (TILE, E), 0)
    for h in range(HEADS):
        cols = head_cols(h)
        tab3 = table_parts(tab_ref[h])
        near_hi, near_lo = hi_lo(near[cols])
        wide_hi, wide_lo = hi_lo(wide[cols])
        state = jnp.concatenate(
            [
                jnp.concatenate([near_hi, wide_hi], axis=1),
                jnp.concatenate([near_lo, wide_lo], axis=1),
            ],
            axis=0,
        )
        a, b = SUMS + h, SUMS + HEADS + h
        ks = jnp.where(row_id == first_lane, near[a : a + 1] + near[b : b + 1], 0.0)
        ks = jnp.where(row_id == first_lane + 1, wide[a : a + 1] + wide[b : b + 1], ks)
        ks = jnp.concatenate(hi_lo(ks), axis=1)
        for i in range(TOK // TILE):
            rows = slice(i * TILE, (i + 1) * TILE)
            qf = feats(q_ref[rows, cols])
            qq = jnp.concatenate([qf, qf], axis=1)
            den = dot_nt(qq, ks)
            through = dot_nn(qq, state)
            coeff = tile_weights(cls_ref[i : i + 1, :], tab3) / jnp.maximum(den, 1.0)
            acc = part_ref[rows, cols]
            acc = acc + coeff[:, first_lane : first_lane + 1] * through[:, :E]
            acc = acc + coeff[:, first_lane + 1 : first_lane + 2] * through[:, E:]
            emit(rows, cols, acc)


def level_kernel(axis, order, first_lane, r_ref, q_ref, cls_ref, tab_ref, part_ref, out_ref):
    def emit(rows, cols, acc):
        out_ref[rows, cols] = acc

    two_levels(axis, order, first_lane, r_ref, q_ref, cls_ref, tab_ref, part_ref, emit)


def final_kernel(axis, order, first_lane, r_ref, q_ref, cls_ref, tab_ref, part_ref, mixed_ref, gated_ref):
    def emit(rows, cols, acc):
        mixed = acc.astype(BF16)
        mixed_ref[rows, cols] = mixed
        gate = 0.5 + 1.0 / (1.0 + jnp.exp(-mixed.astype(F32)))
        gated_ref[rows.start // TILE, :, cols] = (q_ref[rows, cols].astype(F32) * gate).astype(BF16)

    two_levels(axis, order, first_lane, r_ref, q_ref, cls_ref, tab_ref, part_ref, emit)


def window_kernel(xq_ref, k_ref, v_ref, seg_ref, rim1_ref, rim2_ref, out_ref):
    place = (
        (lax.axis_index("x") * 4 + lax.axis_index("zh")) * 4 + lax.axis_index("zl")
    ) * 8 + lax.axis_index("head")
    seg_own = seg_ref[0:1, :].astype(F32)
    seg_q = jnp.transpose(jnp.broadcast_to(seg_own, (TILE, TILE)))
    t_row = lax.broadcasted_iota(jnp.int32, (TILE, TILE), 0)
    s_col = lax.broadcasted_iota(jnp.int32, (TILE, TILE), 1)
    low = -1e30
    seg2 = rim2_ref[TILE : TILE + 1, :TILE].astype(F32)
    seg1 = rim1_ref[TILE : TILE + 1, :TILE].astype(F32)
    bias2 = jnp.where((seg_q == seg2) & (s_col > t_row) & (place >= 2), 0.0, low)
    bias1 = jnp.where((seg_q == seg1) & (place >= 1), 0.0, low)
    bias0 = jnp.where((seg_q == seg_own) & (s_col <= t_row), 0.0, low)
    bias = jnp.concatenate([bias2, bias1, bias0], axis=1)
    scale = E ** (-0.5) * LOG2E
    ones = jnp.ones((3 * TILE, E), BF16)
    for g in range(KVH):
        cols = slice(g * E, (g + 1) * E)
        vcols = slice((KVH + g) * E, (KVH + g + 1) * E)
        keys = jnp.concatenate([rim2_ref[:TILE, cols], rim1_ref[:TILE, cols], k_ref[:, cols]], axis=0)
        vals = jnp.concatenate([rim2_ref[:TILE, vcols], rim1_ref[:TILE, vcols], v_ref[:, cols]], axis=0)
        vals = jnp.concatenate([vals, ones], axis=1)
        for j in range(H // KVH):
            src, part = 2 * g + j // 2, j % 2
            sc = dot_nt(xq_ref[src, :, head_cols(part)], keys) * scale + bias
            top = jnp.max(sc, axis=1, keepdims=True)
            probs = jnp.exp2(sc - top).astype(BF16)
            res = dot_nn(probs, vals)
            head = g * (H // KVH) + j
            out_ref[:, head_cols(head)] = (res[:, :E] / res[:, E:]).astype(BF16)


def call(kernel, out, *args, after=(), aliases=None):
    count = len(args)

    def body(*refs):
        kernel(*refs[:count], *refs[count + len(after) :])

    vmem = pl.BlockSpec(memory_space=pltpu.VMEM)
    return pl.pallas_call(
        body,
        out_shape=out,
        in_specs=[vmem] * count + [pl.BlockSpec(memory_space=pl.ANY)] * len(after),
        input_output_aliases=aliases or {},
        compiler_params=pltpu.CompilerParams(vmem_limit_bytes=32 * 1024 * 1024),
    )(*args, *after)


def span_state(keys, values):
    hbm = pl.BlockSpec(memory_space=pltpu.HBM)
    return pl.pallas_call(
        state_kernel,
        out_shape=jax.ShapeDtypeStruct((4, ROWS, E), BF16),
        in_specs=[hbm, hbm],
        scratch_shapes=[
            pltpu.VMEM((TOK, HEADS * E), BF16),
            pltpu.VMEM((TOK, HEADS * E), BF16),
            pltpu.SemaphoreType.DMA((2, CHUNKS)),
        ],
        compiler_params=pltpu.CompilerParams(vmem_limit_bytes=60 * 1024 * 1024),
    )(keys, values)


def pack_kernel(k_ref, v_ref, seg_ref, out_ref):
    width = KVH * E
    out_ref[:TILE, :width] = k_ref[...]
    out_ref[:TILE, width:] = v_ref[...]
    out_ref[TILE:, :] = jnp.zeros((16, 2 * width), BF16)
    out_ref[TILE:, :TILE] = jnp.broadcast_to(seg_ref[0:1, :].astype(F32), (16, TILE)).astype(BF16)


def pick_kernel(own_ref, got_ref, out_ref):
    first = lax.rem(lax.axis_index("head"), 2) == 0

    @pl.when(first)
    def _():
        out_ref[...] = own_ref[...]

    @pl.when(jnp.logical_not(first))
    def _():
        out_ref[...] = got_ref[...]


def swap(value, axis, order=None):
    groups = None if order is None else [list(order)]
    return lax.all_to_all(value, axis, split_axis=0, concat_axis=0, axis_index_groups=groups, tiled=True)


def local(queries, lin_keys, lin_values, level_class, level_table, win_keys, win_values, seg_ids):
    sds = jax.ShapeDtypeStruct
    levels = level_table.shape[2]
    copies = sds((4, ROWS, E), BF16)
    part_shape = sds((TOK, HEADS * E), F32)
    cls = level_class.reshape(TOK // TILE, TILE)
    tab = jnp.pad(jnp.transpose(level_table, (1, 0, 2)), ((0, 0), (0, 0), (0, E - levels)))
    seg_rows = jnp.broadcast_to(seg_ids[None], (8, TILE))

    sum1 = span_state(lin_keys, lin_values)
    from_zl = swap(sum1, "zl", ZL_ORDER)
    sum4 = call(total_kernel, copies, from_zl)
    from_zh = swap(sum4, "zh", ZH_ORDER)
    part = call(local_kernel, part_shape, queries, lin_keys, lin_values, cls, tab, after=(sum4,))
    part = call(
        functools.partial(level_kernel, "zl", ZL_ORDER, 5), part_shape, from_zl, queries, cls, tab, part, aliases={4: 0}
    )

    sum16 = call(total_kernel, copies, from_zh, after=(part,))
    from_x = swap(sum16, "x")
    rim = sds((TILE + 16, 2 * KVH * E), BF16)
    packed = call(pack_kernel, rim, win_keys, win_values, seg_rows, after=(sum16,))
    flat = ("x", "zh", "zl", "head")
    rim2 = lax.ppermute(packed, flat, [(i, i + 2) for i in range(510)])
    part = call(
        functools.partial(level_kernel, "zh", ZH_ORDER, 7),
        part_shape,
        from_zh,
        queries,
        cls,
        tab,
        part,
        after=(packed,),
        aliases={4: 0},
    )
    mixed, gated = call(
        functools.partial(final_kernel, "x", PLAIN, 9),
        (sds((TOK, HEADS * E), BF16), sds((8, TILE, HEADS * E), BF16)),
        from_x,
        queries,
        cls,
        tab,
        part,
    )
    token_q = swap(gated, "head")
    picked = call(pick_kernel, rim, packed, rim2, after=(gated,))
    rim1 = lax.ppermute(picked, "head", [(i, i ^ 1) for i in range(8)])
    out = call(window_kernel, sds((TILE, H * E), BF16), token_q, win_keys, win_values, seg_rows, rim1, rim2)
    return mixed, out


def solution(mesh):
    grid = Mesh(mesh.devices.reshape(4, 4, 4, 8), ("x", "zh", "zl", "head"))
    ctx = ("x", "zh", "zl")
    both = ("x", "zh", "zl", "head")
    return jax.shard_map(
        local,
        mesh=grid,
        in_specs=(
            P(ctx, "head"),
            P(ctx, "head"),
            P(ctx, "head"),
            P(ctx),
            P(None, "head", None),
            P(both, None),
            P(both, None),
            P(both),
        ),
        out_specs=(P(ctx, "head"), P(both, None)),
        check_vma=False,
    )
```

```python
import functools

import jax
import jax.numpy as jnp
from jax import lax
from jax.experimental import pallas as pl
from jax.experimental.pallas import tpu as pltpu
from jax.sharding import Mesh
from jax.sharding import PartitionSpec as P

H = 16
E = 128
KVH = 4
NCLASS = 16
HEADS = 2
TOK = 1024
TILE = 128
CHUNK = 512
PLAIN = (0, 1, 2, 3)
HEAD_ORDER = (4, 0, 1, 2, 3, 5, 6, 7)
ZL_ORDER = (1, 2, 0, 3)
ZH_ORDER = (2, 0, 1, 3)
CHUNKS = TOK // CHUNK
SUMS = HEADS * E
ROWS = SUMS + 16
F32 = jnp.float32
BF16 = jnp.bfloat16
LOG2E = 1.4426950408889634


def feats(x):
    x = x.astype(F32)
    return jnp.where(x > 0, x + 1.0, jnp.exp(x)).astype(BF16)


def dot_nn(a, b):
    return lax.dot_general(a, b, (((1,), (0,)), ((), ())), preferred_element_type=F32)


def dot_nt(a, b):
    return lax.dot_general(a, b, (((1,), (1,)), ((), ())), preferred_element_type=F32)


def dot_tn(a, b):
    return lax.dot_general(a, b, (((0,), (0,)), ((), ())), preferred_element_type=F32)


def hi_lo(x):
    hi = x.astype(BF16)
    return hi, (x - hi.astype(F32)).astype(BF16)


def head_cols(h):
    return slice(h * E, (h + 1) * E)


def sum_rows(sums):
    row = lax.broadcasted_iota(jnp.int32, (16, E), 0)
    out = jnp.zeros((16, E), F32)
    for h in range(HEADS):
        hi = sums[h].astype(BF16).astype(F32)
        out = jnp.where(row == h, hi, out)
        out = jnp.where(row == HEADS + h, sums[h] - hi, out)
    return out.astype(BF16)


def state_kernel(k_hbm, v_hbm, s_ref, k_ref, v_ref, sems):
    copies = []
    for i in range(CHUNKS):
        rows = slice(i * CHUNK, (i + 1) * CHUNK)
        pair = [
            pltpu.make_async_copy(src.at[rows], dst.at[rows], sems.at[n, i])
            for n, (src, dst) in enumerate(((k_hbm, k_ref), (v_hbm, v_ref)))
        ]
        for copy in pair:
            copy.start()
        copies.append(pair)
    state = [jnp.zeros((E, E), F32) for _ in range(HEADS)]
    sums = [jnp.zeros((8, E), F32) for _ in range(HEADS)]
    for i in range(CHUNKS):
        rows = slice(i * CHUNK, (i + 1) * CHUNK)
        for copy in copies[i]:
            copy.wait()
        for h in range(HEADS):
            kf = feats(k_ref[rows, head_cols(h)])
            state[h] = state[h] + dot_tn(kf, v_ref[rows, head_cols(h)])
            sums[h] = sums[h] + dot_nn(jnp.ones((8, CHUNK), BF16), kf)
    rows = sum_rows([sums[h][0:1] for h in range(HEADS)])
    for copy in range(4):
        for h in range(HEADS):
            s_ref[copy, head_cols(h), :] = state[h].astype(BF16)
        s_ref[copy, SUMS:ROWS, :] = rows


def total_kernel(r_ref, s_ref):
    total = r_ref[0].astype(F32)
    for j in range(1, 4):
        total = total + r_ref[j].astype(F32)
    state = total[:SUMS].astype(BF16)
    tail = total[SUMS:]
    rows = sum_rows([tail[h : h + 1] + tail[HEADS + h : HEADS + h + 1] for h in range(HEADS)])
    for copy in range(4):
        s_ref[copy, :SUMS, :] = state
        s_ref[copy, SUMS:ROWS, :] = rows


def table_parts(tab):
    hi = tab.astype(BF16)
    rest = tab - hi.astype(F32)
    mid = rest.astype(BF16)
    low = (rest - mid.astype(F32)).astype(BF16)
    return jnp.concatenate([hi, mid, low], axis=0)


def tile_weights(cls_row, tab3):
    hot = lax.broadcasted_iota(jnp.int32, (NCLASS, TILE), 0) == cls_row
    hot = jnp.where(hot, 1.0, 0.0).astype(BF16)
    return dot_tn(jnp.concatenate([hot, hot, hot], axis=0), tab3)


def local_kernel(q_ref, k_ref, v_ref, cls_ref, tab_ref, part_ref):
    t_row = lax.broadcasted_iota(jnp.int32, (TILE, TILE), 0)
    s_col = lax.broadcasted_iota(jnp.int32, (TILE, TILE), 1)
    same = (t_row // 64) == (s_col // 64)
    mask0 = same & (s_col <= t_row)
    mask1 = (t_row >= 64) & (s_col < 64)
    lane = s_col
    row_id = t_row
    tiles = TOK // TILE
    for h in range(HEADS):
        cols = head_cols(h)
        tab3 = table_parts(tab_ref[h])
        kf = [feats(k_ref[i * TILE : (i + 1) * TILE, cols]) for i in range(tiles)]
        vt = [v_ref[i * TILE : (i + 1) * TILE, cols] for i in range(tiles)]
        state = [dot_tn(kf[i], vt[i]) for i in range(tiles - 1)]
        ksum = [jnp.sum(kf[i].astype(F32), axis=0, keepdims=True) for i in range(tiles - 1)]
        group = {}
        for level, size in ((2, 1), (3, 2), (4, 4)):
            for first in range(0, tiles, 2 * size):
                st = state[first]
                ks = ksum[first]
                for other in range(first + 1, first + size):
                    st = st + state[other]
                    ks = ks + ksum[other]
                group[level, first] = (jnp.concatenate(hi_lo(st), axis=0), ks)
        for i in range(tiles):
            rows = slice(i * TILE, (i + 1) * TILE)
            qf = feats(q_ref[rows, cols])
            qq = jnp.concatenate([qf, qf], axis=1)
            sc = dot_nt(qf, kf[i])
            s0 = jnp.where(mask0, sc, 0.0)
            s1 = jnp.where(mask1, sc, 0.0)
            den = jnp.where(lane == 0, jnp.sum(s0, axis=1, keepdims=True), 0.0)
            den = jnp.where(lane == 1, jnp.sum(s1, axis=1, keepdims=True), den)
            far = []
            for level, size in ((2, 1), (3, 2), (4, 4)):
                if i & size:
                    far.append((level, group[level, i // (2 * size) * 2 * size]))
            if far:
                ks = jnp.zeros((TILE, E), F32)
                for level, (_, row) in far:
                    ks = jnp.where(row_id == level, row, ks)
                den = den + dot_nt(qq, jnp.concatenate(hi_lo(ks), axis=1))
            coeff = tile_weights(cls_ref[i : i + 1, :], tab3) / jnp.maximum(den, 1.0)
            weight = coeff[:, 0:1] * s0 + coeff[:, 1:2] * s1
            acc = dot_nn(weight.astype(BF16), vt[i])
            for level, (st, _) in far:
                acc = acc + coeff[:, level : level + 1] * dot_nn(qq, st)
            part_ref[rows, cols] = acc


def two_levels(axis, order, first_lane, r_ref, q_ref, cls_ref, tab_ref, part_ref, emit):
    me = lax.axis_index(axis)
    bit0 = (me & 1).astype(F32)
    bit1 = (me >> 1).astype(F32)
    place = [order.index(j) for j in range(4)]
    neighbour = jnp.where(me == 3, place[2], place[0])
    near = r_ref[neighbour].astype(F32) * bit0
    wide = (r_ref[place[0]].astype(F32) + r_ref[place[1]].astype(F32)) * bit1
    row_id = lax.broadcasted_iota(jnp.int32, (TILE, E), 0)
    for h in range(HEADS):
        cols = head_cols(h)
        tab3 = table_parts(tab_ref[h])
        near_hi, near_lo = hi_lo(near[cols])
        wide_hi, wide_lo = hi_lo(wide[cols])
        state = jnp.concatenate(
            [
                jnp.concatenate([near_hi, wide_hi], axis=1),
                jnp.concatenate([near_lo, wide_lo], axis=1),
            ],
            axis=0,
        )
        a, b = SUMS + h, SUMS + HEADS + h
        ks = jnp.where(row_id == first_lane, near[a : a + 1] + near[b : b + 1], 0.0)
        ks = jnp.where(row_id == first_lane + 1, wide[a : a + 1] + wide[b : b + 1], ks)
        ks = jnp.concatenate(hi_lo(ks), axis=1)
        for i in range(TOK // TILE):
            rows = slice(i * TILE, (i + 1) * TILE)
            qf = feats(q_ref[rows, cols])
            qq = jnp.concatenate([qf, qf], axis=1)
            den = dot_nt(qq, ks)
            through = dot_nn(qq, state)
            coeff = tile_weights(cls_ref[i : i + 1, :], tab3) / jnp.maximum(den, 1.0)
            acc = part_ref[rows, cols]
            acc = acc + coeff[:, first_lane : first_lane + 1] * through[:, :E]
            acc = acc + coeff[:, first_lane + 1 : first_lane + 2] * through[:, E:]
            emit(rows, cols, acc)


def level_kernel(axis, order, first_lane, r_ref, q_ref, cls_ref, tab_ref, part_ref, out_ref):
    def emit(rows, cols, acc):
        out_ref[rows, cols] = acc

    two_levels(axis, order, first_lane, r_ref, q_ref, cls_ref, tab_ref, part_ref, emit)


def final_kernel(axis, order, first_lane, r_ref, q_ref, cls_ref, tab_ref, part_ref, mixed_ref, gated_ref):
    def emit(rows, cols, acc):
        mixed = acc.astype(BF16)
        mixed_ref[rows, cols] = mixed
        gate = 1.0 + 0.5 * jnp.tanh(0.5 * mixed.astype(F32))
        gated_ref[HEAD_ORDER.index(rows.start // TILE), :, cols] = (q_ref[rows, cols].astype(F32) * gate).astype(BF16)

    two_levels(axis, order, first_lane, r_ref, q_ref, cls_ref, tab_ref, part_ref, emit)


def window_kernel(xq_ref, k_ref, v_ref, seg_ref, rim1_ref, rim2_ref, out_ref):
    place = (
        (lax.axis_index("x") * 4 + lax.axis_index("zh")) * 4 + lax.axis_index("zl")
    ) * 8 + lax.axis_index("head")
    seg_own = seg_ref[0:1, :].astype(F32)
    seg_q = jnp.transpose(jnp.broadcast_to(seg_own, (TILE, TILE)))
    t_row = lax.broadcasted_iota(jnp.int32, (TILE, TILE), 0)
    s_col = lax.broadcasted_iota(jnp.int32, (TILE, TILE), 1)
    low = -1e30
    seg2 = rim2_ref[TILE : TILE + 1, :TILE].astype(F32)
    seg1 = rim1_ref[TILE : TILE + 1, :TILE].astype(F32)
    bias2 = jnp.where((seg_q == seg2) & (s_col > t_row) & (place >= 2), 0.0, low)
    bias1 = jnp.where((seg_q == seg1) & (place >= 1), 0.0, low)
    bias0 = jnp.where((seg_q == seg_own) & (s_col <= t_row), 0.0, low)
    bias = jnp.concatenate([bias2, bias1, bias0], axis=1)
    scale = E ** (-0.5) * LOG2E
    ones = jnp.ones((3 * TILE, E), BF16)
    for g in range(KVH):
        cols = slice(g * E, (g + 1) * E)
        vcols = slice((KVH + g) * E, (KVH + g + 1) * E)
        keys = jnp.concatenate([rim2_ref[:TILE, cols], rim1_ref[:TILE, cols], k_ref[:, cols]], axis=0)
        vals = jnp.concatenate([rim2_ref[:TILE, vcols], rim1_ref[:TILE, vcols], v_ref[:, cols]], axis=0)
        vals = jnp.concatenate([vals, ones], axis=1)
        for j in range(H // KVH):
            src, part = HEAD_ORDER.index(2 * g + j // 2), j % 2
            sc = dot_nt(xq_ref[src, :, head_cols(part)], keys) * scale + bias
            top = jnp.max(sc, axis=1, keepdims=True)
            probs = jnp.exp2(sc - top).astype(BF16)
            res = dot_nn(probs, vals)
            head = g * (H // KVH) + j
            out_ref[:, head_cols(head)] = (res[:, :E] / res[:, E:]).astype(BF16)


def call(kernel, out, *args, after=(), aliases=None):
    count = len(args)

    def body(*refs):
        kernel(*refs[:count], *refs[count + len(after) :])

    vmem = pl.BlockSpec(memory_space=pltpu.VMEM)
    return pl.pallas_call(
        body,
        out_shape=out,
        in_specs=[vmem] * count + [pl.BlockSpec(memory_space=pl.ANY)] * len(after),
        input_output_aliases=aliases or {},
        compiler_params=pltpu.CompilerParams(vmem_limit_bytes=32 * 1024 * 1024),
    )(*args, *after)


def span_state(keys, values):
    hbm = pl.BlockSpec(memory_space=pltpu.HBM)
    return pl.pallas_call(
        state_kernel,
        out_shape=jax.ShapeDtypeStruct((4, ROWS, E), BF16),
        in_specs=[hbm, hbm],
        scratch_shapes=[
            pltpu.VMEM((TOK, HEADS * E), BF16),
            pltpu.VMEM((TOK, HEADS * E), BF16),
            pltpu.SemaphoreType.DMA((2, CHUNKS)),
        ],
        compiler_params=pltpu.CompilerParams(vmem_limit_bytes=60 * 1024 * 1024),
    )(keys, values)


def pack_kernel(k_ref, v_ref, seg_ref, out_ref):
    width = KVH * E
    out_ref[:TILE, :width] = k_ref[...]
    out_ref[:TILE, width:] = v_ref[...]
    out_ref[TILE:, :] = jnp.zeros((16, 2 * width), BF16)
    out_ref[TILE:, :TILE] = jnp.broadcast_to(seg_ref[0:1, :].astype(F32), (16, TILE)).astype(BF16)


def pick_kernel(own_ref, got_ref, out_ref):
    first = lax.rem(lax.axis_index("head"), 2) == 0

    @pl.when(first)
    def _():
        out_ref[...] = own_ref[...]

    @pl.when(jnp.logical_not(first))
    def _():
        out_ref[...] = got_ref[...]


def swap(value, axis, order=None):
    groups = None if order is None else [list(order)]
    return lax.all_to_all(value, axis, split_axis=0, concat_axis=0, axis_index_groups=groups, tiled=True)


def local(queries, lin_keys, lin_values, level_class, level_table, win_keys, win_values, seg_ids):
    sds = jax.ShapeDtypeStruct
    levels = level_table.shape[2]
    copies = sds((4, ROWS, E), BF16)
    part_shape = sds((TOK, HEADS * E), F32)
    cls = level_class.reshape(TOK // TILE, TILE)
    tab = jnp.pad(jnp.transpose(level_table, (1, 0, 2)), ((0, 0), (0, 0), (0, E - levels)))
    seg_rows = jnp.broadcast_to(seg_ids[None], (8, TILE))

    sum1 = span_state(lin_keys, lin_values)
    from_zl = swap(sum1, "zl", ZL_ORDER)
    sum4 = call(total_kernel, copies, from_zl)
    from_zh = swap(sum4, "zh", ZH_ORDER)
    part = call(local_kernel, part_shape, queries, lin_keys, lin_values, cls, tab, after=(sum4,))
    part = call(
        functools.partial(level_kernel, "zl", ZL_ORDER, 5), part_shape, from_zl, queries, cls, tab, part, aliases={4: 0}
    )

    sum16 = call(total_kernel, copies, from_zh, after=(part,))
    from_x = swap(sum16, "x")
    rim = sds((TILE + 16, 2 * KVH * E), BF16)
    packed = call(pack_kernel, rim, win_keys, win_values, seg_rows, after=(sum16,))
    flat = ("x", "zh", "zl", "head")
    rim2 = lax.ppermute(packed, flat, [(i, i + 2) for i in range(510)])
    part = call(
        functools.partial(level_kernel, "zh", ZH_ORDER, 7),
        part_shape,
        from_zh,
        queries,
        cls,
        tab,
        part,
        after=(packed,),
        aliases={4: 0},
    )
    mixed, gated = call(
        functools.partial(final_kernel, "x", PLAIN, 9),
        (sds((TOK, HEADS * E), BF16), sds((8, TILE, HEADS * E), BF16)),
        from_x,
        queries,
        cls,
        tab,
        part,
    )
    token_q = swap(gated, "head", HEAD_ORDER)
    picked = call(pick_kernel, rim, packed, rim2, after=(gated,))
    rim1 = lax.ppermute(picked, "head", [(i, i ^ 1) for i in range(8)])
    out = call(window_kernel, sds((TILE, H * E), BF16), token_q, win_keys, win_values, seg_rows, rim1, rim2)
    return mixed, out


def solution(mesh):
    grid = Mesh(mesh.devices.reshape(4, 4, 4, 8), ("x", "zh", "zl", "head"))
    ctx = ("x", "zh", "zl")
    both = ("x", "zh", "zl", "head")
    return jax.shard_map(
        local,
        mesh=grid,
        in_specs=(
            P(ctx, "head"),
            P(ctx, "head"),
            P(ctx, "head"),
            P(ctx),
            P(None, "head", None),
            P(both, None),
            P(both, None),
            P(both),
        ),
        out_specs=(P(ctx, "head"), P(both, None)),
        check_vma=False,
    )
```

```python
import functools

import jax
import jax.numpy as jnp
from jax import lax
from jax.experimental import pallas as pl
from jax.experimental.pallas import tpu as pltpu
from jax.sharding import Mesh
from jax.sharding import PartitionSpec as P

H = 16
E = 128
KVH = 4
NCLASS = 16
HEADS = 2
TOK = 1024
TILE = 128
CHUNK = 512
PLAIN = (0, 1, 2, 3)
HEAD_ORDER = (4, 0, 1, 2, 3, 5, 6, 7)
ZL_ORDER = (2, 1, 0, 3)
ZH_ORDER = (2, 0, 3, 1)
CHUNKS = TOK // CHUNK
SUMS = HEADS * E
ROWS = SUMS + 16
F32 = jnp.float32
BF16 = jnp.bfloat16
LOG2E = 1.4426950408889634


def feats(x):
    x = x.astype(F32)
    return jnp.where(x > 0, x + 1.0, jnp.exp(x)).astype(BF16)


def dot_nn(a, b):
    return lax.dot_general(a, b, (((1,), (0,)), ((), ())), preferred_element_type=F32)


def dot_nt(a, b):
    return lax.dot_general(a, b, (((1,), (1,)), ((), ())), preferred_element_type=F32)


def dot_tn(a, b):
    return lax.dot_general(a, b, (((0,), (0,)), ((), ())), preferred_element_type=F32)


def hi_lo(x):
    hi = x.astype(BF16)
    return hi, (x - hi.astype(F32)).astype(BF16)


def head_cols(h):
    return slice(h * E, (h + 1) * E)


def sum_rows(sums):
    row = lax.broadcasted_iota(jnp.int32, (16, E), 0)
    out = jnp.zeros((16, E), F32)
    for h in range(HEADS):
        hi = sums[h].astype(BF16).astype(F32)
        out = jnp.where(row == h, hi, out)
        out = jnp.where(row == HEADS + h, sums[h] - hi, out)
    return out.astype(BF16)


def state_kernel(k_hbm, v_hbm, s_ref, k_ref, v_ref, sems):
    copies = []
    for i in range(CHUNKS):
        rows = slice(i * CHUNK, (i + 1) * CHUNK)
        pair = [
            pltpu.make_async_copy(src.at[rows], dst.at[rows], sems.at[n, i])
            for n, (src, dst) in enumerate(((k_hbm, k_ref), (v_hbm, v_ref)))
        ]
        for copy in pair:
            copy.start()
        copies.append(pair)
    state = [jnp.zeros((E, E), F32) for _ in range(HEADS)]
    sums = [jnp.zeros((8, E), F32) for _ in range(HEADS)]
    for i in range(CHUNKS):
        rows = slice(i * CHUNK, (i + 1) * CHUNK)
        for copy in copies[i]:
            copy.wait()
        for h in range(HEADS):
            kf = feats(k_ref[rows, head_cols(h)])
            state[h] = state[h] + dot_tn(kf, v_ref[rows, head_cols(h)])
            sums[h] = sums[h] + dot_nn(jnp.ones((8, CHUNK), BF16), kf)
    rows = sum_rows([sums[h][0:1] for h in range(HEADS)])
    for copy in range(4):
        for h in range(HEADS):
            s_ref[copy, head_cols(h), :] = state[h].astype(BF16)
        s_ref[copy, SUMS:ROWS, :] = rows


def total_kernel(r_ref, s_ref):
    total = r_ref[0].astype(F32)
    for j in range(1, 4):
        total = total + r_ref[j].astype(F32)
    state = total[:SUMS].astype(BF16)
    tail = total[SUMS:]
    rows = sum_rows([tail[h : h + 1] + tail[HEADS + h : HEADS + h + 1] for h in range(HEADS)])
    for copy in range(4):
        s_ref[copy, :SUMS, :] = state
        s_ref[copy, SUMS:ROWS, :] = rows


def table_parts(tab):
    hi = tab.astype(BF16)
    rest = tab - hi.astype(F32)
    mid = rest.astype(BF16)
    low = (rest - mid.astype(F32)).astype(BF16)
    return jnp.concatenate([hi, mid, low], axis=0)


def tile_weights(cls_row, tab3):
    hot = lax.broadcasted_iota(jnp.int32, (NCLASS, TILE), 0) == cls_row
    hot = jnp.where(hot, 1.0, 0.0).astype(BF16)
    return dot_tn(jnp.concatenate([hot, hot, hot], axis=0), tab3)


def local_kernel(q_ref, k_ref, v_ref, cls_ref, tab_ref, part_ref):
    t_row = lax.broadcasted_iota(jnp.int32, (TILE, TILE), 0)
    s_col = lax.broadcasted_iota(jnp.int32, (TILE, TILE), 1)
    same = (t_row // 64) == (s_col // 64)
    mask0 = same & (s_col <= t_row)
    mask1 = (t_row >= 64) & (s_col < 64)
    lane = s_col
    row_id = t_row
    tiles = TOK // TILE
    for h in range(HEADS):
        cols = head_cols(h)
        tab3 = table_parts(tab_ref[h])
        kf = [feats(k_ref[i * TILE : (i + 1) * TILE, cols]) for i in range(tiles)]
        vt = [v_ref[i * TILE : (i + 1) * TILE, cols] for i in range(tiles)]
        state = [dot_tn(kf[i], vt[i]) for i in range(tiles - 1)]
        ksum = [jnp.sum(kf[i].astype(F32), axis=0, keepdims=True) for i in range(tiles - 1)]
        group = {}
        for level, size in ((2, 1), (3, 2), (4, 4)):
            for first in range(0, tiles, 2 * size):
                st = state[first]
                ks = ksum[first]
                for other in range(first + 1, first + size):
                    st = st + state[other]
                    ks = ks + ksum[other]
                group[level, first] = (jnp.concatenate(hi_lo(st), axis=0), ks)
        for i in range(tiles):
            rows = slice(i * TILE, (i + 1) * TILE)
            qf = feats(q_ref[rows, cols])
            qq = jnp.concatenate([qf, qf], axis=1)
            sc = dot_nt(qf, kf[i])
            s0 = jnp.where(mask0, sc, 0.0)
            s1 = jnp.where(mask1, sc, 0.0)
            den = jnp.where(lane == 0, jnp.sum(s0, axis=1, keepdims=True), 0.0)
            den = jnp.where(lane == 1, jnp.sum(s1, axis=1, keepdims=True), den)
            far = []
            for level, size in ((2, 1), (3, 2), (4, 4)):
                if i & size:
                    far.append((level, group[level, i // (2 * size) * 2 * size]))
            if far:
                ks = jnp.zeros((TILE, E), F32)
                for level, (_, row) in far:
                    ks = jnp.where(row_id == level, row, ks)
                den = den + dot_nt(qq, jnp.concatenate(hi_lo(ks), axis=1))
            coeff = tile_weights(cls_ref[i : i + 1, :], tab3) / jnp.maximum(den, 1.0)
            weight = coeff[:, 0:1] * s0 + coeff[:, 1:2] * s1
            acc = dot_nn(weight.astype(BF16), vt[i])
            for level, (st, _) in far:
                acc = acc + coeff[:, level : level + 1] * dot_nn(qq, st)
            part_ref[rows, cols] = acc


def two_levels(axis, order, first_lane, r_ref, q_ref, cls_ref, tab_ref, part_ref, emit):
    me = lax.axis_index(axis)
    bit0 = (me & 1).astype(F32)
    bit1 = (me >> 1).astype(F32)
    place = [order.index(j) for j in range(4)]
    neighbour = jnp.where(me == 3, place[2], place[0])
    near = r_ref[neighbour].astype(F32) * bit0
    wide = (r_ref[place[0]].astype(F32) + r_ref[place[1]].astype(F32)) * bit1
    row_id = lax.broadcasted_iota(jnp.int32, (TILE, E), 0)
    for h in range(HEADS):
        cols = head_cols(h)
        tab3 = table_parts(tab_ref[h])
        near_hi, near_lo = hi_lo(near[cols])
        wide_hi, wide_lo = hi_lo(wide[cols])
        state = jnp.concatenate(
            [
                jnp.concatenate([near_hi, wide_hi], axis=1),
                jnp.concatenate([near_lo, wide_lo], axis=1),
            ],
            axis=0,
        )
        a, b = SUMS + h, SUMS + HEADS + h
        ks = jnp.where(row_id == first_lane, near[a : a + 1] + near[b : b + 1], 0.0)
        ks = jnp.where(row_id == first_lane + 1, wide[a : a + 1] + wide[b : b + 1], ks)
        ks = jnp.concatenate(hi_lo(ks), axis=1)
        for i in range(TOK // TILE):
            rows = slice(i * TILE, (i + 1) * TILE)
            qf = feats(q_ref[rows, cols])
            qq = jnp.concatenate([qf, qf], axis=1)
            den = dot_nt(qq, ks)
            through = dot_nn(qq, state)
            coeff = tile_weights(cls_ref[i : i + 1, :], tab3) / jnp.maximum(den, 1.0)
            acc = part_ref[rows, cols]
            acc = acc + coeff[:, first_lane : first_lane + 1] * through[:, :E]
            acc = acc + coeff[:, first_lane + 1 : first_lane + 2] * through[:, E:]
            emit(rows, cols, acc)


def level_kernel(axis, order, first_lane, r_ref, q_ref, cls_ref, tab_ref, part_ref, out_ref):
    def emit(rows, cols, acc):
        out_ref[rows, cols] = acc

    two_levels(axis, order, first_lane, r_ref, q_ref, cls_ref, tab_ref, part_ref, emit)


def final_kernel(axis, order, first_lane, r_ref, q_ref, cls_ref, tab_ref, part_ref, mixed_ref, gated_ref):
    def emit(rows, cols, acc):
        mixed = acc.astype(BF16)
        mixed_ref[rows, cols] = mixed
        gate = 1.0 + 0.5 * jnp.tanh(0.5 * mixed.astype(F32))
        gated_ref[HEAD_ORDER.index(rows.start // TILE), :, cols] = (q_ref[rows, cols].astype(F32) * gate).astype(BF16)

    two_levels(axis, order, first_lane, r_ref, q_ref, cls_ref, tab_ref, part_ref, emit)


def window_kernel(xq_ref, k_ref, v_ref, seg_ref, rim1_ref, rim2_ref, out_ref):
    place = (
        (lax.axis_index("x") * 4 + lax.axis_index("zh")) * 4 + lax.axis_index("zl")
    ) * 8 + lax.axis_index("head")
    seg_own = seg_ref[0:1, :].astype(F32)
    seg_q = jnp.transpose(jnp.broadcast_to(seg_own, (TILE, TILE)))
    t_row = lax.broadcasted_iota(jnp.int32, (TILE, TILE), 0)
    s_col = lax.broadcasted_iota(jnp.int32, (TILE, TILE), 1)
    low = -1e30
    seg2 = rim2_ref[TILE : TILE + 1, :TILE].astype(F32)
    seg1 = rim1_ref[TILE : TILE + 1, :TILE].astype(F32)
    bias2 = jnp.where((seg_q == seg2) & (s_col > t_row) & (place >= 2), 0.0, low)
    bias1 = jnp.where((seg_q == seg1) & (place >= 1), 0.0, low)
    bias0 = jnp.where((seg_q == seg_own) & (s_col <= t_row), 0.0, low)
    bias = jnp.concatenate([bias2, bias1, bias0], axis=1)
    scale = E ** (-0.5) * LOG2E
    ones = jnp.ones((3 * TILE, E), BF16)
    for g in range(KVH):
        cols = slice(g * E, (g + 1) * E)
        vcols = slice((KVH + g) * E, (KVH + g + 1) * E)
        keys = jnp.concatenate([rim2_ref[:TILE, cols], rim1_ref[:TILE, cols], k_ref[:, cols]], axis=0)
        vals = jnp.concatenate([rim2_ref[:TILE, vcols], rim1_ref[:TILE, vcols], v_ref[:, cols]], axis=0)
        vals = jnp.concatenate([vals, ones], axis=1)
        for j in range(H // KVH):
            src, part = HEAD_ORDER.index(2 * g + j // 2), j % 2
            sc = dot_nt(xq_ref[src, :, head_cols(part)], keys) * scale + bias
            top = jnp.max(sc, axis=1, keepdims=True)
            probs = jnp.exp2(sc - top).astype(BF16)
            res = dot_nn(probs, vals)
            head = g * (H // KVH) + j
            out_ref[:, head_cols(head)] = (res[:, :E] / res[:, E:]).astype(BF16)


def call(kernel, out, *args, after=(), aliases=None):
    count = len(args)

    def body(*refs):
        kernel(*refs[:count], *refs[count + len(after) :])

    vmem = pl.BlockSpec(memory_space=pltpu.VMEM)
    return pl.pallas_call(
        body,
        out_shape=out,
        in_specs=[vmem] * count + [pl.BlockSpec(memory_space=pl.ANY)] * len(after),
        input_output_aliases=aliases or {},
        compiler_params=pltpu.CompilerParams(vmem_limit_bytes=32 * 1024 * 1024),
    )(*args, *after)


def span_state(keys, values):
    hbm = pl.BlockSpec(memory_space=pltpu.HBM)
    return pl.pallas_call(
        state_kernel,
        out_shape=jax.ShapeDtypeStruct((4, ROWS, E), BF16),
        in_specs=[hbm, hbm],
        scratch_shapes=[
            pltpu.VMEM((TOK, HEADS * E), BF16),
            pltpu.VMEM((TOK, HEADS * E), BF16),
            pltpu.SemaphoreType.DMA((2, CHUNKS)),
        ],
        compiler_params=pltpu.CompilerParams(vmem_limit_bytes=60 * 1024 * 1024),
    )(keys, values)


def pack_kernel(k_ref, v_ref, seg_ref, out_ref):
    width = KVH * E
    out_ref[:TILE, :width] = k_ref[...]
    out_ref[:TILE, width:] = v_ref[...]
    out_ref[TILE:, :] = jnp.zeros((16, 2 * width), BF16)
    out_ref[TILE:, :TILE] = jnp.broadcast_to(seg_ref[0:1, :].astype(F32), (16, TILE)).astype(BF16)


def pick_kernel(own_ref, got_ref, out_ref):
    first = lax.rem(lax.axis_index("head"), 2) == 0

    @pl.when(first)
    def _():
        out_ref[...] = own_ref[...]

    @pl.when(jnp.logical_not(first))
    def _():
        out_ref[...] = got_ref[...]


def swap(value, axis, order=None):
    groups = None if order is None else [list(order)]
    return lax.all_to_all(value, axis, split_axis=0, concat_axis=0, axis_index_groups=groups, tiled=True)


def local(queries, lin_keys, lin_values, level_class, level_table, win_keys, win_values, seg_ids):
    sds = jax.ShapeDtypeStruct
    levels = level_table.shape[2]
    copies = sds((4, ROWS, E), BF16)
    part_shape = sds((TOK, HEADS * E), F32)
    cls = level_class.reshape(TOK // TILE, TILE)
    tab = jnp.pad(jnp.transpose(level_table, (1, 0, 2)), ((0, 0), (0, 0), (0, E - levels)))
    seg_rows = jnp.broadcast_to(seg_ids[None], (8, TILE))

    sum1 = span_state(lin_keys, lin_values)
    from_zl = swap(sum1, "zl", ZL_ORDER)
    sum4 = call(total_kernel, copies, from_zl)
    from_zh = swap(sum4, "zh", ZH_ORDER)
    part = call(local_kernel, part_shape, queries, lin_keys, lin_values, cls, tab, after=(sum4,))
    part = call(
        functools.partial(level_kernel, "zl", ZL_ORDER, 5), part_shape, from_zl, queries, cls, tab, part, aliases={4: 0}
    )

    sum16 = call(total_kernel, copies, from_zh, after=(part,))
    from_x = swap(sum16, "x")
    rim = sds((TILE + 16, 2 * KVH * E), BF16)
    packed = call(pack_kernel, rim, win_keys, win_values, seg_rows, after=(sum16,))
    flat = ("x", "zh", "zl", "head")
    rim2 = lax.ppermute(packed, flat, [(i, i + 2) for i in range(510)])
    part = call(
        functools.partial(level_kernel, "zh", ZH_ORDER, 7),
        part_shape,
        from_zh,
        queries,
        cls,
        tab,
        part,
        after=(packed,),
        aliases={4: 0},
    )
    mixed, gated = call(
        functools.partial(final_kernel, "x", PLAIN, 9),
        (sds((TOK, HEADS * E), BF16), sds((8, TILE, HEADS * E), BF16)),
        from_x,
        queries,
        cls,
        tab,
        part,
    )
    token_q = swap(gated, "head", HEAD_ORDER)
    picked = call(pick_kernel, rim, packed, rim2, after=(gated,))
    rim1 = lax.ppermute(picked, "head", [(i, i ^ 1) for i in range(8)])
    out = call(window_kernel, sds((TILE, H * E), BF16), token_q, win_keys, win_values, seg_rows, rim1, rim2)
    return mixed, out


def solution(mesh):
    grid = Mesh(mesh.devices.reshape(4, 4, 4, 8), ("x", "zh", "zl", "head"))
    ctx = ("x", "zh", "zl")
    both = ("x", "zh", "zl", "head")
    return jax.shard_map(
        local,
        mesh=grid,
        in_specs=(
            P(ctx, "head"),
            P(ctx, "head"),
            P(ctx, "head"),
            P(ctx),
            P(None, "head", None),
            P(both, None),
            P(both, None),
            P(both),
        ),
        out_specs=(P(ctx, "head"), P(both, None)),
        check_vma=False,
    )
```

```python
import functools

import jax
import jax.numpy as jnp
from jax import lax
from jax.experimental import pallas as pl
from jax.experimental.pallas import tpu as pltpu
from jax.sharding import Mesh
from jax.sharding import PartitionSpec as P

H = 16
E = 128
KVH = 4
NCLASS = 16
HEADS = 2
TOK = 1024
TILE = 128
CHUNK = 512
PLAIN = (0, 1, 2, 3)
HEAD_ORDER = (4, 0, 1, 2, 3, 5, 6, 7)
ZL_ORDER = (2, 0, 3, 1)
ZH_ORDER = (2, 0, 3, 1)
CHUNKS = TOK // CHUNK
SUMS = HEADS * E
ROWS = SUMS + 16
F32 = jnp.float32
BF16 = jnp.bfloat16
LOG2E = 1.4426950408889634


def feats(x):
    x = x.astype(F32)
    return jnp.where(x > 0, x + 1.0, jnp.exp(x)).astype(BF16)


def dot_nn(a, b):
    return lax.dot_general(a, b, (((1,), (0,)), ((), ())), preferred_element_type=F32)


def dot_nt(a, b):
    return lax.dot_general(a, b, (((1,), (1,)), ((), ())), preferred_element_type=F32)


def dot_tn(a, b):
    return lax.dot_general(a, b, (((0,), (0,)), ((), ())), preferred_element_type=F32)


def hi_lo(x):
    hi = x.astype(BF16)
    return hi, (x - hi.astype(F32)).astype(BF16)


def head_cols(h):
    return slice(h * E, (h + 1) * E)


def sum_rows(sums):
    row = lax.broadcasted_iota(jnp.int32, (16, E), 0)
    out = jnp.zeros((16, E), F32)
    for h in range(HEADS):
        hi = sums[h].astype(BF16).astype(F32)
        out = jnp.where(row == h, hi, out)
        out = jnp.where(row == HEADS + h, sums[h] - hi, out)
    return out.astype(BF16)


def state_kernel(k_hbm, v_hbm, s_ref, k_ref, v_ref, sems):
    copies = []
    for i in range(CHUNKS):
        rows = slice(i * CHUNK, (i + 1) * CHUNK)
        pair = [
            pltpu.make_async_copy(src.at[rows], dst.at[rows], sems.at[n, i])
            for n, (src, dst) in enumerate(((k_hbm, k_ref), (v_hbm, v_ref)))
        ]
        for copy in pair:
            copy.start()
        copies.append(pair)
    state = [jnp.zeros((E, E), F32) for _ in range(HEADS)]
    sums = [jnp.zeros((8, E), F32) for _ in range(HEADS)]
    for i in range(CHUNKS):
        rows = slice(i * CHUNK, (i + 1) * CHUNK)
        for copy in copies[i]:
            copy.wait()
        for h in range(HEADS):
            kf = feats(k_ref[rows, head_cols(h)])
            state[h] = state[h] + dot_tn(kf, v_ref[rows, head_cols(h)])
            sums[h] = sums[h] + dot_nn(jnp.ones((8, CHUNK), BF16), kf)
    rows = sum_rows([sums[h][0:1] for h in range(HEADS)])
    for copy in range(4):
        for h in range(HEADS):
            s_ref[copy, head_cols(h), :] = state[h].astype(BF16)
        s_ref[copy, SUMS:ROWS, :] = rows


def total_kernel(r_ref, s_ref):
    total = r_ref[0].astype(F32)
    for j in range(1, 4):
        total = total + r_ref[j].astype(F32)
    state = total[:SUMS].astype(BF16)
    tail = total[SUMS:]
    rows = sum_rows([tail[h : h + 1] + tail[HEADS + h : HEADS + h + 1] for h in range(HEADS)])
    for copy in range(4):
        s_ref[copy, :SUMS, :] = state
        s_ref[copy, SUMS:ROWS, :] = rows


def table_parts(tab):
    hi = tab.astype(BF16)
    rest = tab - hi.astype(F32)
    mid = rest.astype(BF16)
    low = (rest - mid.astype(F32)).astype(BF16)
    return jnp.concatenate([hi, mid, low], axis=0)


def tile_weights(cls_row, tab3):
    hot = lax.broadcasted_iota(jnp.int32, (NCLASS, TILE), 0) == cls_row
    hot = jnp.where(hot, 1.0, 0.0).astype(BF16)
    return dot_tn(jnp.concatenate([hot, hot, hot], axis=0), tab3)


def local_kernel(q_ref, k_ref, v_ref, cls_ref, tab_ref, part_ref):
    t_row = lax.broadcasted_iota(jnp.int32, (TILE, TILE), 0)
    s_col = lax.broadcasted_iota(jnp.int32, (TILE, TILE), 1)
    same = (t_row // 64) == (s_col // 64)
    mask0 = same & (s_col <= t_row)
    mask1 = (t_row >= 64) & (s_col < 64)
    lane = s_col
    row_id = t_row
    tiles = TOK // TILE
    for h in range(HEADS):
        cols = head_cols(h)
        tab3 = table_parts(tab_ref[h])
        kf = [feats(k_ref[i * TILE : (i + 1) * TILE, cols]) for i in range(tiles)]
        vt = [v_ref[i * TILE : (i + 1) * TILE, cols] for i in range(tiles)]
        state = [dot_tn(kf[i], vt[i]) for i in range(tiles - 1)]
        ksum = [jnp.sum(kf[i].astype(F32), axis=0, keepdims=True) for i in range(tiles - 1)]
        group = {}
        for level, size in ((2, 1), (3, 2), (4, 4)):
            for first in range(0, tiles, 2 * size):
                st = state[first]
                ks = ksum[first]
                for other in range(first + 1, first + size):
                    st = st + state[other]
                    ks = ks + ksum[other]
                group[level, first] = (jnp.concatenate(hi_lo(st), axis=0), ks)
        for i in range(tiles):
            rows = slice(i * TILE, (i + 1) * TILE)
            qf = feats(q_ref[rows, cols])
            qq = jnp.concatenate([qf, qf], axis=1)
            sc = dot_nt(qf, kf[i])
            s0 = jnp.where(mask0, sc, 0.0)
            s1 = jnp.where(mask1, sc, 0.0)
            den = jnp.where(lane == 0, jnp.sum(s0, axis=1, keepdims=True), 0.0)
            den = jnp.where(lane == 1, jnp.sum(s1, axis=1, keepdims=True), den)
            far = []
            for level, size in ((2, 1), (3, 2), (4, 4)):
                if i & size:
                    far.append((level, group[level, i // (2 * size) * 2 * size]))
            if far:
                ks = jnp.zeros((TILE, E), F32)
                for level, (_, row) in far:
                    ks = jnp.where(row_id == level, row, ks)
                den = den + dot_nt(qq, jnp.concatenate(hi_lo(ks), axis=1))
            coeff = tile_weights(cls_ref[i : i + 1, :], tab3) / jnp.maximum(den, 1.0)
            weight = coeff[:, 0:1] * s0 + coeff[:, 1:2] * s1
            acc = dot_nn(weight.astype(BF16), vt[i])
            for level, (st, _) in far:
                acc = acc + coeff[:, level : level + 1] * dot_nn(qq, st)
            part_ref[rows, cols] = acc


def two_levels(axis, order, first_lane, r_ref, q_ref, cls_ref, tab_ref, part_ref, emit):
    me = lax.axis_index(axis)
    bit0 = (me & 1).astype(F32)
    bit1 = (me >> 1).astype(F32)
    place = [order.index(j) for j in range(4)]
    neighbour = jnp.where(me == 3, place[2], place[0])
    near = r_ref[neighbour].astype(F32) * bit0
    wide = (r_ref[place[0]].astype(F32) + r_ref[place[1]].astype(F32)) * bit1
    row_id = lax.broadcasted_iota(jnp.int32, (TILE, E), 0)
    for h in range(HEADS):
        cols = head_cols(h)
        tab3 = table_parts(tab_ref[h])
        near_hi, near_lo = hi_lo(near[cols])
        wide_hi, wide_lo = hi_lo(wide[cols])
        state = jnp.concatenate(
            [
                jnp.concatenate([near_hi, wide_hi], axis=1),
                jnp.concatenate([near_lo, wide_lo], axis=1),
            ],
            axis=0,
        )
        a, b = SUMS + h, SUMS + HEADS + h
        ks = jnp.where(row_id == first_lane, near[a : a + 1] + near[b : b + 1], 0.0)
        ks = jnp.where(row_id == first_lane + 1, wide[a : a + 1] + wide[b : b + 1], ks)
        ks = jnp.concatenate(hi_lo(ks), axis=1)
        for i in range(TOK // TILE):
            rows = slice(i * TILE, (i + 1) * TILE)
            qf = feats(q_ref[rows, cols])
            qq = jnp.concatenate([qf, qf], axis=1)
            den = dot_nt(qq, ks)
            through = dot_nn(qq, state)
            coeff = tile_weights(cls_ref[i : i + 1, :], tab3) / jnp.maximum(den, 1.0)
            acc = part_ref[rows, cols]
            acc = acc + coeff[:, first_lane : first_lane + 1] * through[:, :E]
            acc = acc + coeff[:, first_lane + 1 : first_lane + 2] * through[:, E:]
            emit(rows, cols, acc)


def level_kernel(axis, order, first_lane, r_ref, q_ref, cls_ref, tab_ref, part_ref, out_ref):
    def emit(rows, cols, acc):
        out_ref[rows, cols] = acc

    two_levels(axis, order, first_lane, r_ref, q_ref, cls_ref, tab_ref, part_ref, emit)


def final_kernel(axis, order, first_lane, r_ref, q_ref, cls_ref, tab_ref, part_ref, mixed_ref, gated_ref):
    def emit(rows, cols, acc):
        mixed = acc.astype(BF16)
        mixed_ref[rows, cols] = mixed
        gate = 1.0 + 0.5 * jnp.tanh(0.5 * mixed.astype(F32))
        gated_ref[HEAD_ORDER.index(rows.start // TILE), :, cols] = (q_ref[rows, cols].astype(F32) * gate).astype(BF16)

    two_levels(axis, order, first_lane, r_ref, q_ref, cls_ref, tab_ref, part_ref, emit)


def prepare_kernel(k_ref, v_ref, seg_ref, rim1_ref, rim2_ref, bias_ref, keys_ref, vals_ref):
    place = (
        (lax.axis_index("x") * 4 + lax.axis_index("zh")) * 4 + lax.axis_index("zl")
    ) * 8 + lax.axis_index("head")
    seg_own = seg_ref[0:1, :].astype(F32)
    seg_q = jnp.transpose(jnp.broadcast_to(seg_own, (TILE, TILE)))
    t_row = lax.broadcasted_iota(jnp.int32, (TILE, TILE), 0)
    s_col = lax.broadcasted_iota(jnp.int32, (TILE, TILE), 1)
    low = -1e30
    seg2 = rim2_ref[TILE : TILE + 1, :TILE].astype(F32)
    seg1 = rim1_ref[TILE : TILE + 1, :TILE].astype(F32)
    bias_ref[:, :TILE] = jnp.where((seg_q == seg2) & (s_col > t_row) & (place >= 2), 0.0, low)
    bias_ref[:, TILE : 2 * TILE] = jnp.where((seg_q == seg1) & (place >= 1), 0.0, low)
    bias_ref[:, 2 * TILE :] = jnp.where((seg_q == seg_own) & (s_col <= t_row), 0.0, low)
    for g in range(KVH):
        cols = slice(g * E, (g + 1) * E)
        vcols = slice((KVH + g) * E, (KVH + g + 1) * E)
        keys_ref[g, :TILE] = rim2_ref[:TILE, cols]
        keys_ref[g, TILE : 2 * TILE] = rim1_ref[:TILE, cols]
        keys_ref[g, 2 * TILE :] = k_ref[:, cols]
        vals_ref[g, :TILE, :E] = rim2_ref[:TILE, vcols]
        vals_ref[g, TILE : 2 * TILE, :E] = rim1_ref[:TILE, vcols]
        vals_ref[g, 2 * TILE :, :E] = v_ref[:, cols]
        vals_ref[g, :, E:] = jnp.ones((3 * TILE, E), BF16)


def window_kernel(xq_ref, bias_ref, keys_ref, vals_ref, out_hbm, out_ref, sems):
    scale = E ** (-0.5) * LOG2E
    bias = bias_ref[...]
    copies = []
    for g in range(KVH):
        keys = keys_ref[g]
        vals = vals_ref[g]
        for j in range(H // KVH):
            src, part = HEAD_ORDER.index(2 * g + j // 2), j % 2
            sc = dot_nt(xq_ref[src, :, head_cols(part)], keys) * scale + bias
            top = jnp.max(sc, axis=1, keepdims=True)
            probs = jnp.exp2(sc - top).astype(BF16)
            res = dot_nn(probs, vals)
            head = g * (H // KVH) + j
            out_ref[:, head_cols(head)] = (res[:, :E] / res[:, E:]).astype(BF16)
        cols = slice(g * E * (H // KVH), (g + 1) * E * (H // KVH))
        copies.append(pltpu.make_async_copy(out_ref.at[:, cols], out_hbm.at[:, cols], sems.at[g]))
        copies[g].start()
    for copy in copies:
        copy.wait()


def window(token_q, bias, keys, vals):
    vmem = pl.BlockSpec(memory_space=pltpu.VMEM)
    return pl.pallas_call(
        window_kernel,
        out_shape=jax.ShapeDtypeStruct((TILE, H * E), BF16),
        in_specs=[vmem] * 4,
        out_specs=pl.BlockSpec(memory_space=pltpu.HBM),
        scratch_shapes=[pltpu.VMEM((TILE, H * E), BF16), pltpu.SemaphoreType.DMA((KVH,))],
        compiler_params=pltpu.CompilerParams(vmem_limit_bytes=32 * 1024 * 1024),
    )(token_q, bias, keys, vals)


def call(kernel, out, *args, after=(), aliases=None):
    count = len(args)

    def body(*refs):
        kernel(*refs[:count], *refs[count + len(after) :])

    vmem = pl.BlockSpec(memory_space=pltpu.VMEM)
    return pl.pallas_call(
        body,
        out_shape=out,
        in_specs=[vmem] * count + [pl.BlockSpec(memory_space=pl.ANY)] * len(after),
        input_output_aliases=aliases or {},
        compiler_params=pltpu.CompilerParams(vmem_limit_bytes=32 * 1024 * 1024),
    )(*args, *after)


def span_state(keys, values):
    hbm = pl.BlockSpec(memory_space=pltpu.HBM)
    return pl.pallas_call(
        state_kernel,
        out_shape=jax.ShapeDtypeStruct((4, ROWS, E), BF16),
        in_specs=[hbm, hbm],
        scratch_shapes=[
            pltpu.VMEM((TOK, HEADS * E), BF16),
            pltpu.VMEM((TOK, HEADS * E), BF16),
            pltpu.SemaphoreType.DMA((2, CHUNKS)),
        ],
        compiler_params=pltpu.CompilerParams(vmem_limit_bytes=60 * 1024 * 1024),
    )(keys, values)


def pack_kernel(k_ref, v_ref, seg_ref, out_ref):
    width = KVH * E
    out_ref[:TILE, :width] = k_ref[...]
    out_ref[:TILE, width:] = v_ref[...]
    out_ref[TILE:, :] = jnp.zeros((16, 2 * width), BF16)
    out_ref[TILE:, :TILE] = jnp.broadcast_to(seg_ref[0:1, :].astype(F32), (16, TILE)).astype(BF16)


def pick_kernel(own_ref, got_ref, out_ref):
    first = lax.rem(lax.axis_index("head"), 2) == 0

    @pl.when(first)
    def _():
        out_ref[...] = own_ref[...]

    @pl.when(jnp.logical_not(first))
    def _():
        out_ref[...] = got_ref[...]


def swap(value, axis, order=None):
    groups = None if order is None else [list(order)]
    return lax.all_to_all(value, axis, split_axis=0, concat_axis=0, axis_index_groups=groups, tiled=True)


def local(queries, lin_keys, lin_values, level_class, level_table, win_keys, win_values, seg_ids):
    sds = jax.ShapeDtypeStruct
    levels = level_table.shape[2]
    copies = sds((4, ROWS, E), BF16)
    part_shape = sds((TOK, HEADS * E), F32)
    cls = level_class.reshape(TOK // TILE, TILE)
    tab = jnp.pad(jnp.transpose(level_table, (1, 0, 2)), ((0, 0), (0, 0), (0, E - levels)))
    seg_rows = jnp.broadcast_to(seg_ids[None], (8, TILE))

    sum1 = span_state(lin_keys, lin_values)
    from_zl = swap(sum1, "zl", ZL_ORDER)
    sum4 = call(total_kernel, copies, from_zl)
    from_zh = swap(sum4, "zh", ZH_ORDER)
    part = call(local_kernel, part_shape, queries, lin_keys, lin_values, cls, tab, after=(sum4,))
    part = call(
        functools.partial(level_kernel, "zl", ZL_ORDER, 5), part_shape, from_zl, queries, cls, tab, part, aliases={4: 0}
    )

    rim = sds((TILE + 16, 2 * KVH * E), BF16)
    packed = call(pack_kernel, rim, win_keys, win_values, seg_rows, after=(sum4,))
    sum16 = call(total_kernel, copies, from_zh, after=(part, packed))
    from_x = swap(sum16, "x")
    packed, sum16 = lax.optimization_barrier((packed, sum16))
    flat = ("x", "zh", "zl", "head")
    rim2 = lax.ppermute(packed, flat, [(i, i + 2) for i in range(510)])
    part = call(
        functools.partial(level_kernel, "zh", ZH_ORDER, 7),
        part_shape,
        from_zh,
        queries,
        cls,
        tab,
        part,
        after=(sum16,),
        aliases={4: 0},
    )
    mixed, gated = call(
        functools.partial(final_kernel, "x", PLAIN, 9),
        (sds((TOK, HEADS * E), BF16), sds((8, TILE, HEADS * E), BF16)),
        from_x,
        queries,
        cls,
        tab,
        part,
    )
    token_q = swap(gated, "head", HEAD_ORDER)
    picked = call(pick_kernel, rim, packed, rim2, after=(gated,))
    rim1 = lax.ppermute(picked, "head", [(i, i ^ 1) for i in range(8)])
    laid = call(
        prepare_kernel,
        (sds((TILE, 3 * TILE), F32), sds((KVH, 3 * TILE, E), BF16), sds((KVH, 3 * TILE, 2 * E), BF16)),
        win_keys,
        win_values,
        seg_rows,
        rim1,
        rim2,
    )
    return mixed, window(token_q, *laid)


def solution(mesh):
    grid = Mesh(mesh.devices.reshape(4, 4, 4, 8), ("x", "zh", "zl", "head"))
    ctx = ("x", "zh", "zl")
    both = ("x", "zh", "zl", "head")
    return jax.shard_map(
        local,
        mesh=grid,
        in_specs=(
            P(ctx, "head"),
            P(ctx, "head"),
            P(ctx, "head"),
            P(ctx),
            P(None, "head", None),
            P(both, None),
            P(both, None),
            P(both),
        ),
        out_specs=(P(ctx, "head"), P(both, None)),
        check_vma=False,
    )
```
